256 devices in a mesh: dp: 32 (over z, x), mp: 8 (over y, core).
Axes of the slice: x: 4, y: 4, z: 8, core: 2. Of those that a mesh axis runs over, the one named last changes fastest.
Arguments:
- grads: bfloat16 [32, 256, 28672], P('dp', None, 'mp'), may hold values from -6 to 6
- errors: float32 [32, 256, 28672], P('dp', None, 'mp'), may hold values from -4 to 4
- q_init: float32 [28672, 32], P('mp'), may hold values from -6 to 6
Outputs:
- update: bfloat16 [256, 28672], P(None, 'mp')
- new_errors: float32 [32, 256, 28672], P('dp', None, 'mp')
- q_next: float32 [28672, 32], P('mp')
The draws below stay inside these ranges and needn't reach their ends.
All inputs are finite; a program needn't handle non-finite values.
Results may differ from the reference program's by a relative error of at most 0.001.
Values sent between devices are 32-bit elements; how exact they have to be, the bound alone decides.
A program may use at most 64 MiB of HBM per device.

```python
import jax
import jax.numpy as jnp
from jax import lax

ROWS = 256
FF = 28672
RANK = 32
REPLICAS = 32
N_DP = 32


def shard_levels(stream_key, dims, cuts, least, largest):
    loudness = 1.0
    for position, blocks in cuts:
        draws = jax.random.uniform(jax.random.fold_in(jax.random.fold_in(stream_key, 6), position), (blocks,), jnp.float32, least / len(cuts), largest / len(cuts))
        loudness = loudness * jnp.repeat(jnp.exp(draws), dims[position] // blocks).reshape((-1,) + (1,) * (len(dims) - 1 - position))
    return loudness


def bell_draw(stream_key, extent, width, limit, split=(), held_as=jnp.bfloat16):
    level = shard_levels(stream_key, extent, split, -0.22, 0.18) if split else 1.0
    result = jax.random.normal(stream_key, extent, jnp.float32) * width * level
    return jnp.minimum(jnp.maximum(result, -limit), limit).astype(held_as)


def setup_inputs(seed: int = 0) -> dict:
    key_list = jax.random.split(jax.random.key(seed), 4)
    grads = bell_draw(key_list[0], (REPLICAS, ROWS, FF), 1.0, 6.0, ((0, 32), (2, 8)))
    errors = bell_draw(key_list[1], (REPLICAS, ROWS, FF), 0.5, 4.0, ((0, 32), (2, 8)), jnp.float32)
    q_init = bell_draw(key_list[2], (FF, RANK), 1.0, 6.0, ((0, 8),), jnp.float32)
    return {"grads": grads, "errors": errors, "q_init": q_init}


def orthonormal(p_sum):
    gram = jnp.dot(p_sum.T, p_sum, precision=lax.Precision.HIGHEST)
    lower = jnp.linalg.cholesky(gram)
    return jax.scipy.linalg.solve_triangular(lower, p_sum.T, lower=True).T

def reference(grads, errors, q_init):

    def p_step(total, pair):
        merged = pair[0].astype(jnp.float32) + pair[1]
        return (total + jnp.dot(merged, q_init, precision=lax.Precision.HIGHEST), None)
    p_sum, unused = lax.scan(p_step, jnp.zeros((ROWS, RANK), jnp.float32), (grads, errors))
    p_hat = orthonormal(p_sum)

    def q_step(total, pair):
        merged = pair[0].astype(jnp.float32) + pair[1]
        return (total + jnp.dot(merged.T, p_hat, precision=lax.Precision.HIGHEST), None)
    q_total, unused = lax.scan(q_step, jnp.zeros((FF, RANK), jnp.float32), (grads, errors))
    q_next = q_total / N_DP
    recon = jnp.dot(p_hat, q_next.T, precision=lax.Precision.HIGHEST)
    update = recon.astype(jnp.bfloat16)
    new_errors = grads.astype(jnp.float32) + errors - recon[None]
    return (update, new_errors, q_next)
```

```python
import functools

import jax
import jax.numpy as jnp
from jax import lax
from jax.experimental import pallas as pl
from jax.experimental.pallas import tpu as pltpu
from jax.sharding import PartitionSpec as P

MESH = pl.DeviceIdType.MESH
HIGHEST = lax.Precision.HIGHEST
F32 = jnp.float32
BF16 = jnp.bfloat16

NZ, NX, NMP = 8, 4, 8
ROWS, RANK = 256, 32
VMEM = pl.BlockSpec(memory_space=pltpu.VMEM)
ANY = pl.BlockSpec(memory_space=pl.ANY)


def ring_hops(offset, size):
    return min(offset, size - offset)


Z_OFFSETS = sorted(range(1, NZ), key=lambda d: -ring_hops(d, NZ))
X_OFFSETS = sorted(range(1, NX), key=lambda d: -ring_hops(d, NX))
DP_OFFSETS = sorted(
    ((dz, dx) for dz in range(NZ) for dx in range(NX) if dz or dx),
    key=lambda d: -(ring_hops(d[0], NZ) + ring_hops(d[1], NX)),
)
MP_OFFSETS = [4, 5, 2, 6, 3, 7, 1]


def split(value):
    high = value.astype(BF16)
    return high, (value - high.astype(F32)).astype(BF16)


def dot_t(a, b):
    return lax.dot_general(a, b, (((1,), (1,)), ((), ())), preferred_element_type=F32)


def inverse_factor(gram):
    rows = lax.broadcasted_iota(jnp.int32, (RANK, 4 * RANK), 0)
    lanes = lax.broadcasted_iota(jnp.int32, (RANK, 4 * RANK), 1)
    work = jnp.where(lanes == rows + RANK, 1.0, 0.0)
    work = work + jnp.concatenate([gram, jnp.zeros((RANK, 3 * RANK), F32)], axis=1)
    for k in range(RANK):
        row = work[k : k + 1, :]
        pivot = work[k : k + 1, k : k + 1]
        column = work[:, k : k + 1]
        scale = lax.rsqrt(pivot)
        row = row * scale
        step = work - (column * scale) * row
        below = rows > k
        work = jnp.where(below, step, jnp.where(rows == k, row, work))
    return work[:, RANK : 2 * RANK]


def reduce_kernel(
    g_hbm, e_hbm, qt_hbm, q_out, inv_out, phat_out,
    g_v, e_v, qt_v, high_v, low_v, p_loc, p_rs, p_ar, p_all,
    x_src, x_buf, z_src, z_buf, ag,
    load_sem, p_send, p_recv, x_send, x_recv, z_send, z_recv, ag_send, agz_recv, agx_recv,
):
    dp, mp = lax.axis_index("dp"), lax.axis_index("mp")
    z, x = dp // NX, lax.rem(dp, NX)
    width = g_v.shape[2]

    def z_peer(d):
        return lax.rem(z + d, NZ)

    def x_peer(d):
        return lax.rem(x + d, NX)

    def dp_peer(dz, dx):
        return z_peer(dz) * NX + x_peer(dx)

    def mp_peer(d):
        return lax.rem(mp + d, NMP)

    def send(src, dst, send_sem, recv_sem, dp_to, mp_to):
        pltpu.make_async_remote_copy(
            src_ref=src, dst_ref=dst, send_sem=send_sem, recv_sem=recv_sem,
            device_id=(dp_to, mp_to), device_id_type=MESH,
        ).start()

    def wait_bytes(ref, sem):
        pltpu.make_async_copy(ref, ref, sem).wait()

    loads = []
    for i in range(NX):
        cols = pl.ds(i * width, width)
        three = [
            pltpu.make_async_copy(g_hbm.at[0, :, cols], g_v.at[i], load_sem.at[0, i]),
            pltpu.make_async_copy(e_hbm.at[0, :, cols], e_v.at[i], load_sem.at[1, i]),
            pltpu.make_async_copy(qt_hbm.at[:, cols], qt_v.at[i], load_sem.at[2, i]),
        ]
        for copy in three:
            copy.start()
        loads.append(three)

    barrier = pltpu.get_barrier_semaphore()
    for dz, dx in DP_OFFSETS:
        pl.semaphore_signal(barrier, inc=1, device_id=(dp_peer(dz, dx), mp), device_id_type=MESH)
    for d in MP_OFFSETS:
        pl.semaphore_signal(barrier, inc=1, device_id=(dp, mp_peer(d)), device_id_type=MESH)

    p_part = jnp.zeros((ROWS, 2 * RANK), F32)
    for i in range(NX):
        for copy in loads[i]:
            copy.wait()
        high, low = split(g_v[i].astype(F32) + e_v[i])
        high_v[i] = high
        low_v[i] = low
        q_both = jnp.concatenate(split(qt_v[i]), axis=0)
        p_part += dot_t(high, q_both) + dot_t(low, q_both)
    p_t = (p_part[:, :RANK] + p_part[:, RANK:]).T
    for t in range(NMP):
        p_loc[t] = p_t[8 * (t % 4) : 8 * (t % 4) + 8, 128 * (t // 4) : 128 * (t // 4) + 128]

    pl.semaphore_wait(barrier, len(DP_OFFSETS) + len(MP_OFFSETS))

    for d in MP_OFFSETS:
        to = mp_peer(d)
        send(p_loc.at[to], p_rs.at[mp], p_send.at[0], p_recv.at[0], dp, to)
    p_rs[mp] = p_loc[mp]
    wait_bytes(p_rs.at[pl.ds(0, NMP - 1)], p_recv.at[0])
    p_ar[dp] = jnp.sum(p_rs[...], axis=0)
    for dz, dx in DP_OFFSETS:
        send(p_ar.at[dp], p_ar.at[dp], p_send.at[1], p_recv.at[1], dp_peer(dz, dx), mp)
    wait_bytes(p_ar.at[pl.ds(0, NZ * NX - 1)], p_recv.at[1])
    p_all[mp] = jnp.sum(p_ar[...], axis=0)
    for d in MP_OFFSETS:
        send(p_all.at[mp], p_all.at[mp], p_send.at[2], p_recv.at[2], dp, mp_peer(d))
    wait_bytes(p_all.at[pl.ds(0, NMP - 1)], p_recv.at[2])
    p_t = jnp.concatenate(
        [
            jnp.concatenate([p_all[t] for t in range(4)], axis=0),
            jnp.concatenate([p_all[t] for t in range(4, 8)], axis=0),
        ],
        axis=1,
    )

    p_high, p_low = split(p_t)
    p_both = jnp.concatenate([p_high, p_low], axis=0)
    for d in X_OFFSETS + [0]:
        to = x_peer(d)
        first = jnp.dot(p_both, high_v[to], preferred_element_type=F32)
        second = jnp.dot(p_high, low_v[to], preferred_element_type=F32)
        block = first[:RANK] + first[RANK:] + second
        if d:
            x_src[to] = block
            send(x_src.at[to], x_buf.at[x], x_send, x_recv, z * NX + to, mp)
        else:
            x_buf[x] = block

    gram = lax.dot_general(
        p_t, p_t, (((1,), (1,)), ((), ())), precision=HIGHEST, preferred_element_type=F32
    )
    inverse = inverse_factor(gram)
    inv_out[...] = inverse
    phat_out[...] = jnp.dot(inverse, p_t, precision=HIGHEST, preferred_element_type=F32).T

    wait_bytes(x_buf.at[pl.ds(0, NX - 1)], x_recv)
    block = jnp.sum(x_buf[...], axis=0)
    rows = RANK // NZ
    for i in range(NZ):
        z_src[i] = block[i * rows : (i + 1) * rows]
    for d in Z_OFFSETS:
        to = z_peer(d)
        send(z_src.at[to], z_buf.at[z], z_send, z_recv, to * NX + x, mp)
    z_buf[z] = z_src[z]
    wait_bytes(z_buf.at[pl.ds(0, NZ - 1)], z_recv)
    ag[x, z] = jnp.sum(z_buf[...], axis=0)

    for d in Z_OFFSETS:
        send(ag.at[x, z], ag.at[x, z], ag_send, agz_recv.at[z], z_peer(d) * NX + x, mp)
    for d in [0] + Z_OFFSETS[::-1]:
        at = z_peer(d)
        if d:
            wait_bytes(ag.at[x, at], agz_recv.at[at])
        for dx in X_OFFSETS:
            send(ag.at[x, at], ag.at[x, at], ag_send, agx_recv, z * NX + x_peer(dx), mp)
    wait_bytes(ag.at[pl.ds(0, NX - 1)], agx_recv)
    for i in range(NX):
        q_out[:, i * width : (i + 1) * width] = jnp.concatenate(
            [ag[i, j] for j in range(NZ)], axis=0
        )

    wait_bytes(p_rs.at[pl.ds(0, NMP - 1)], p_send.at[0])
    wait_bytes(p_ar.at[pl.ds(0, NZ * NX - 1)], p_send.at[1])
    wait_bytes(p_all.at[pl.ds(0, NMP - 1)], p_send.at[2])
    wait_bytes(x_buf.at[pl.ds(0, NX - 1)], x_send)
    wait_bytes(z_buf.at[pl.ds(0, NZ - 1)], z_send)
    wait_bytes(ag.at[pl.ds(0, NX - 1)], ag_send)
    wait_bytes(ag.at[0, pl.ds(0, NZ - 1)], ag_send)


def finish_kernel(replicas, g_ref, e_ref, q_ref, inv_ref, phat_ref, u_ref, n_ref, q_out):
    q_next = jnp.dot(inv_ref[...], q_ref[...], precision=HIGHEST, preferred_element_type=F32)
    q_next = q_next * (1.0 / replicas)
    q_out[...] = q_next
    p_high, p_low = split(phat_ref[...])
    q_high, q_low = split(q_next)
    left = jnp.concatenate([p_high, p_low, p_high, p_low], axis=1)
    right = jnp.concatenate([q_high, q_high, q_low, q_low], axis=0)
    recon = jnp.dot(left, right, preferred_element_type=F32)
    u_ref[...] = recon.astype(BF16)
    n_ref[0] = g_ref[0].astype(F32) + e_ref[0] - recon


def body(grads, errors, q_init):
    columns = grads.shape[2]
    width = columns // NX
    piece = RANK // NZ
    dma = pltpu.SemaphoreType.DMA
    q_sum, inverse, p_hat = pl.pallas_call(
        reduce_kernel,
        out_shape=(
            jax.ShapeDtypeStruct((RANK, columns), F32),
            jax.ShapeDtypeStruct((RANK, RANK), F32),
            jax.ShapeDtypeStruct((ROWS, RANK), F32),
        ),
        in_specs=[ANY] * 3,
        out_specs=[VMEM] * 3,
        scratch_shapes=[
            pltpu.VMEM((NX, ROWS, width), BF16),
            pltpu.VMEM((NX, ROWS, width), F32),
            pltpu.VMEM((NX, RANK, width), F32),
            pltpu.VMEM((NX, ROWS, width), BF16),
            pltpu.VMEM((NX, ROWS, width), BF16),
            pltpu.VMEM((NMP, 8, 128), F32),
            pltpu.VMEM((NMP, 8, 128), F32),
            pltpu.VMEM((NZ * NX, 8, 128), F32),
            pltpu.VMEM((NMP, 8, 128), F32),
            pltpu.VMEM((NX, RANK, width), F32),
            pltpu.VMEM((NX, RANK, width), F32),
            pltpu.VMEM((NZ, piece, width), F32),
            pltpu.VMEM((NZ, piece, width), F32),
            pltpu.VMEM((NX, NZ, piece, width), F32),
            dma((3, NX)),
            dma((3,)),
            dma((3,)),
            dma,
            dma,
            dma,
            dma,
            dma,
            dma((NZ,)),
            dma,
        ],
        compiler_params=pltpu.CompilerParams(
            collective_id=0, has_side_effects=True, vmem_limit_bytes=40 << 20
        ),
        name="reduce",
    )(grads, errors, q_init.T)

    block = 512
    update, new_errors, q_next = pl.pallas_call(
        functools.partial(finish_kernel, lax.axis_size("dp")),
        grid=(columns // block,),
        out_shape=(
            jax.ShapeDtypeStruct((ROWS, columns), BF16),
            jax.ShapeDtypeStruct((1, ROWS, columns), F32),
            jax.ShapeDtypeStruct((RANK, columns), F32),
        ),
        in_specs=[
            pl.BlockSpec((1, ROWS, block), lambda j: (0, 0, j)),
            pl.BlockSpec((1, ROWS, block), lambda j: (0, 0, j)),
            pl.BlockSpec((RANK, block), lambda j: (0, j)),
            pl.BlockSpec((RANK, RANK), lambda j: (0, 0)),
            pl.BlockSpec((ROWS, RANK), lambda j: (0, 0)),
        ],
        out_specs=(
            pl.BlockSpec((ROWS, block), lambda j: (0, j)),
            pl.BlockSpec((1, ROWS, block), lambda j: (0, 0, j)),
            pl.BlockSpec((RANK, block), lambda j: (0, j)),
        ),
        compiler_params=pltpu.CompilerParams(vmem_limit_bytes=32 << 20),
        name="finish",
    )(grads, errors, q_sum, inverse, p_hat)
    return (update, new_errors, q_next.T)


def solution(mesh):
    placed = (P("dp", None, "mp"), P("dp", None, "mp"), P("mp", None))
    return jax.shard_map(
        body,
        mesh=mesh,
        in_specs=placed,
        out_specs=(P(None, "mp"), P("dp", None, "mp"), P("mp", None)),
        check_vma=False,
    )
```

```python
import functools

import jax
import jax.numpy as jnp
from jax import lax
from jax.experimental import pallas as pl
from jax.experimental.pallas import tpu as pltpu
from jax.sharding import PartitionSpec as P

MESH = pl.DeviceIdType.MESH
HIGHEST = lax.Precision.HIGHEST
F32 = jnp.float32
BF16 = jnp.bfloat16

NZ, NX, NMP = 8, 4, 8
ROWS, RANK = 256, 32
VMEM = pl.BlockSpec(memory_space=pltpu.VMEM)
HBM = pl.BlockSpec(memory_space=pltpu.HBM)


def around(i, size):
    half = (i + 1) // 2
    return lax.rem(size // 2 + jnp.where(lax.rem(i, 2) == 0, half, size - half), size)


def split(value):
    high = value.astype(BF16)
    return high, (value - high.astype(F32)).astype(BF16)


def split3(value):
    high = value.astype(BF16)
    middle, low = split(value - high.astype(F32))
    return high, middle, low


def stack_left(value):
    h, m, l = split3(value)
    return jnp.concatenate([h, h, m, h, m, l], axis=1)


def stack_right(value):
    h, m, l = split3(value)
    return jnp.concatenate([h, m, h, l, m, h], axis=0)


def dot_t(a, b):
    return lax.dot_general(a, b, (((1,), (1,)), ((), ())), preferred_element_type=F32)


def inverse_factor(gram):
    rows = lax.broadcasted_iota(jnp.int32, (RANK, 4 * RANK), 0)
    lanes = lax.broadcasted_iota(jnp.int32, (RANK, 4 * RANK), 1)
    work = jnp.where(lanes == rows + RANK, 1.0, 0.0)
    work = work + jnp.concatenate([gram, jnp.zeros((RANK, 3 * RANK), F32)], axis=1)
    for k in range(RANK):
        row = work[k : k + 1, :]
        pivot = work[k : k + 1, k : k + 1]
        column = work[:, k : k + 1]
        scale = lax.rsqrt(pivot)
        row = row * scale
        step = work - (column * scale) * row
        below = rows > k
        work = jnp.where(below, step, jnp.where(rows == k, row, work))
    return work[:, RANK : 2 * RANK]


def reduce_kernel(
    g_hbm, e_hbm, qt_hbm, merged_out, q_out, inv_out, phat_out,
    g_v, e_v, qt_v, high_v, low_v, p_acc, p_loc, p_rs, p_ar, p_all,
    x_src, x_buf, z_src, z_buf, ag,
    load_sem, p_send, p_recv, x_send, x_recv, z_send, z_recv, ag_send, agz_recv, agx_recv,
):
    dp, mp = lax.axis_index("dp"), lax.axis_index("mp")
    z, x = dp // NX, lax.rem(dp, NX)
    y, core = mp // 2, lax.rem(mp, 2)
    width = g_v.shape[2]
    n_dp = NZ * NX

    def z_peer(i):
        return lax.rem(z + around(i, NZ), NZ)

    def x_peer(i):
        return lax.rem(x + around(i, NX), NX)

    def dp_peer(i):
        return z_peer(i // NX) * NX + x_peer(lax.rem(i, NX))

    def mp_peer(i):
        return lax.rem(y + around(i // 2, NMP // 2), NMP // 2) * 2 + lax.rem(core + i + 1, 2)

    def each(n, act):
        lax.fori_loop(0, n, lambda i, c: (act(i), c)[1], 0)

    def send(src, dst, send_sem, recv_sem, dp_to, mp_to):
        pltpu.make_async_remote_copy(
            src_ref=src, dst_ref=dst, send_sem=send_sem, recv_sem=recv_sem,
            device_id=(dp_to, mp_to), device_id_type=MESH,
        ).start()

    def wait_bytes(ref, sem):
        pltpu.make_async_copy(ref, ref, sem).wait()

    def loads(i):
        cols = pl.ds(pl.multiple_of(i * width, 128), width)
        return (
            pltpu.make_async_copy(qt_hbm.at[:, cols], qt_v.at[i], load_sem.at[2, i]),
            pltpu.make_async_copy(g_hbm.at[0, :, cols], g_v.at[i], load_sem.at[0, i]),
            pltpu.make_async_copy(e_hbm.at[0, :, cols], e_v.at[i], load_sem.at[1, i]),
        )

    @functools.partial(each, NX)
    def _(i):
        for copy in loads(i):
            copy.start()

    barrier = pltpu.get_barrier_semaphore()

    @functools.partial(each, n_dp - 1)
    def _(i):
        pl.semaphore_signal(barrier, inc=1, device_id=(dp_peer(i), mp), device_id_type=MESH)

    @functools.partial(each, NMP - 1)
    def _(i):
        pl.semaphore_signal(barrier, inc=1, device_id=(dp, mp_peer(i)), device_id_type=MESH)

    drain = []

    p_acc[...] = jnp.zeros_like(p_acc)

    @functools.partial(each, NX)
    def _(i):
        for copy in loads(i):
            copy.wait()
        merged = g_v[i].astype(F32) + e_v[i]
        merged_out[i] = merged
        high, low = split(merged)
        high_v[i] = high
        low_v[i] = low
        q_both = jnp.concatenate(split(qt_v[i]), axis=0)
        p_acc[...] += dot_t(high, q_both) + dot_t(low, q_both)

    p_t = (p_acc[:, :RANK] + p_acc[:, RANK:]).T
    for t in range(NMP):
        p_loc[t] = p_t[8 * (t % 4) : 8 * (t % 4) + 8, 128 * (t // 4) : 128 * (t // 4) + 128]

    pl.semaphore_wait(barrier, n_dp - 1 + NMP - 1)

    @functools.partial(each, NMP - 1)
    def _(i):
        to = mp_peer(i)
        send(p_loc.at[to], p_rs.at[mp], p_send.at[0], p_recv.at[0], dp, to)

    drain.append((p_rs.at[pl.ds(0, NMP - 1)], p_send.at[0]))
    p_rs[mp] = p_loc[mp]
    wait_bytes(p_rs.at[pl.ds(0, NMP - 1)], p_recv.at[0])
    p_ar[dp] = jnp.sum(p_rs[...], axis=0)

    @functools.partial(each, n_dp - 1)
    def _(i):
        send(p_ar.at[dp], p_ar.at[dp], p_send.at[1], p_recv.at[1], dp_peer(i), mp)

    drain.append((p_ar.at[pl.ds(0, n_dp - 1)], p_send.at[1]))
    wait_bytes(p_ar.at[pl.ds(0, n_dp - 1)], p_recv.at[1])
    p_all[mp] = jnp.sum(p_ar[...], axis=0)

    @functools.partial(each, NMP - 1)
    def _(i):
        send(p_all.at[mp], p_all.at[mp], p_send.at[2], p_recv.at[2], dp, mp_peer(i))

    drain.append((p_all.at[pl.ds(0, NMP - 1)], p_send.at[2]))
    wait_bytes(p_all.at[pl.ds(0, NMP - 1)], p_recv.at[2])
    p_t = jnp.concatenate(
        [
            jnp.concatenate([p_all[t] for t in range(4)], axis=0),
            jnp.concatenate([p_all[t] for t in range(4, 8)], axis=0),
        ],
        axis=1,
    )

    p_both = jnp.concatenate(split(p_t), axis=0)

    @functools.partial(each, NX)
    def _(i):
        to = x_peer(i)
        both = jnp.dot(p_both, high_v[to], preferred_element_type=F32)
        both += jnp.dot(p_both, low_v[to], preferred_element_type=F32)
        x_src[to] = both[:RANK] + both[RANK:]

        @pl.when(i < NX - 1)
        def _():
            send(x_src.at[to], x_buf.at[x], x_send, x_recv, z * NX + to, mp)

    drain.append((x_buf.at[pl.ds(0, NX - 1)], x_send))
    x_buf[x] = x_src[x]

    gram = lax.dot_general(
        p_t, p_t, (((1,), (1,)), ((), ())), precision=HIGHEST, preferred_element_type=F32
    )
    inverse = inverse_factor(gram)
    inv_out[...] = stack_left(inverse)
    phat_out[...] = stack_left(
        jnp.dot(inverse, p_t, precision=HIGHEST, preferred_element_type=F32).T
    )

    wait_bytes(x_buf.at[pl.ds(0, NX - 1)], x_recv)
    block = jnp.sum(x_buf[...], axis=0)
    rows = RANK // NZ
    for i in range(NZ):
        z_src[i] = block[i * rows : (i + 1) * rows]

    @functools.partial(each, NZ - 1)
    def _(i):
        to = z_peer(i)
        send(z_src.at[to], z_buf.at[z], z_send, z_recv, to * NX + x, mp)

    drain.append((z_buf.at[pl.ds(0, NZ - 1)], z_send))
    z_buf[z] = z_src[z]
    wait_bytes(z_buf.at[pl.ds(0, NZ - 1)], z_recv)
    ag[x, z] = jnp.sum(z_buf[...], axis=0)

    @functools.partial(each, NZ - 1)
    def _(i):
        send(ag.at[x, z], ag.at[x, z], ag_send, agz_recv.at[z], z_peer(i) * NX + x, mp)

    @functools.partial(each, NZ)
    def _(i):
        at = z_peer(NZ - 1 - i)

        @pl.when(i > 0)
        def _():
            wait_bytes(ag.at[x, at], agz_recv.at[at])

        @functools.partial(each, NX - 1)
        def _(j):
            send(ag.at[x, at], ag.at[x, at], ag_send, agx_recv, z * NX + x_peer(j), mp)

    drain.append((ag.at[pl.ds(0, NX - 1)], ag_send))
    drain.append((ag.at[0, pl.ds(0, NZ - 1)], ag_send))
    wait_bytes(ag.at[pl.ds(0, NX - 1)], agx_recv)
    for i in range(NX):
        q_out[i] = jnp.concatenate([ag[i, j] for j in range(NZ)], axis=0)

    for ref, sem in drain:
        wait_bytes(ref, sem)


def finish_kernel(
    replicas, merged_ref, q_ref, inv_ref, phat_ref, u_hbm, n_hbm, q_hbm, u_v, n_v, q_v, sems
):
    blocks, _, width = merged_ref.shape
    half = ROWS // 2

    def block(i, carry):
        cols = pl.ds(pl.multiple_of(i * width, 128), width)
        q_next = jnp.dot(inv_ref[...], stack_right(q_ref[i]), preferred_element_type=F32)
        q_next = q_next * (1.0 / replicas)
        q_v[i] = q_next
        pltpu.make_async_copy(q_v.at[i], q_hbm.at[:, cols], sems.at[0]).start()
        right = stack_right(q_next)
        for h in range(2):
            rows = slice(h * half, (h + 1) * half)
            at = pl.ds(h * half, half)
            recon = jnp.dot(phat_ref[rows], right, preferred_element_type=F32)
            n_v[i, rows] = merged_ref[i, rows] - recon
            pltpu.make_async_copy(n_v.at[i, at], n_hbm.at[0, at, cols], sems.at[1]).start()
            u_v[i, rows] = recon.astype(BF16)
            pltpu.make_async_copy(u_v.at[i, at], u_hbm.at[at, cols], sems.at[2]).start()
        return carry

    lax.fori_loop(0, blocks, block, 0)
    for ref, sem in ((q_v, sems.at[0]), (n_v, sems.at[1]), (u_v, sems.at[2])):
        pltpu.make_async_copy(ref, ref, sem).wait()


def body(grads, errors, q_init):
    columns = grads.shape[2]
    width = columns // NX
    piece = RANK // NZ
    dma = pltpu.SemaphoreType.DMA
    held = pl.pallas_call(
        reduce_kernel,
        out_shape=(
            jax.ShapeDtypeStruct((NX, ROWS, width), F32),
            jax.ShapeDtypeStruct((NX, RANK, width), F32),
            jax.ShapeDtypeStruct((RANK, 6 * RANK), BF16),
            jax.ShapeDtypeStruct((ROWS, 6 * RANK), BF16),
        ),
        in_specs=[HBM] * 3,
        out_specs=[VMEM] * 4,
        scratch_shapes=[
            pltpu.VMEM((NX, ROWS, width), BF16),
            pltpu.VMEM((NX, ROWS, width), F32),
            pltpu.VMEM((NX, RANK, width), F32),
            pltpu.VMEM((NX, ROWS, width), BF16),
            pltpu.VMEM((NX, ROWS, width), BF16),
            pltpu.VMEM((ROWS, 2 * RANK), F32),
            pltpu.VMEM((NMP, 8, 128), F32),
            pltpu.VMEM((NMP, 8, 128), F32),
            pltpu.VMEM((NZ * NX, 8, 128), F32),
            pltpu.VMEM((NMP, 8, 128), F32),
            pltpu.VMEM((NX, RANK, width), F32),
            pltpu.VMEM((NX, RANK, width), F32),
            pltpu.VMEM((NZ, piece, width), F32),
            pltpu.VMEM((NZ, piece, width), F32),
            pltpu.VMEM((NX, NZ, piece, width), F32),
            dma((3, NX)),
            dma((3,)),
            dma((3,)),
            dma,
            dma,
            dma,
            dma,
            dma,
            dma((NZ,)),
            dma,
        ],
        compiler_params=pltpu.CompilerParams(
            collective_id=0, has_side_effects=True, vmem_limit_bytes=40 << 20
        ),
        name="reduce",
    )(*(pltpu.with_memory_space_constraint(a, pltpu.HBM) for a in (grads, errors, q_init.T)))

    update, new_errors, q_next = pl.pallas_call(
        functools.partial(finish_kernel, lax.axis_size("dp")),
        out_shape=(
            jax.ShapeDtypeStruct((ROWS, columns), BF16),
            jax.ShapeDtypeStruct((1, ROWS, columns), F32),
            jax.ShapeDtypeStruct((RANK, columns), F32),
        ),
        in_specs=[VMEM] * 4,
        out_specs=[HBM] * 3,
        scratch_shapes=[
            pltpu.VMEM((NX, ROWS, width), BF16),
            pltpu.VMEM((NX, ROWS, width), F32),
            pltpu.VMEM((NX, RANK, width), F32),
            dma((3,)),
        ],
        compiler_params=pltpu.CompilerParams(vmem_limit_bytes=32 << 20),
        name="finish",
    )(*held)
    return (update, new_errors, q_next.T)


def solution(mesh):
    placed = (P("dp", None, "mp"), P("dp", None, "mp"), P("mp", None))
    return jax.shard_map(
        body,
        mesh=mesh,
        in_specs=placed,
        out_specs=(P(None, "mp"), P("dp", None, "mp"), P("mp", None)),
        check_vma=False,
    )
```

```python
import functools

import jax
import jax.numpy as jnp
from jax import lax
from jax.experimental import pallas as pl
from jax.experimental.pallas import tpu as pltpu
from jax.sharding import PartitionSpec as P

MESH = pl.DeviceIdType.MESH
HIGHEST = lax.Precision.HIGHEST
F32 = jnp.float32
BF16 = jnp.bfloat16

NZ, NX, NMP = 8, 4, 8
ROWS, RANK = 256, 32
VMEM = pl.BlockSpec(memory_space=pltpu.VMEM)
HBM = pl.BlockSpec(memory_space=pltpu.HBM)


def around(i, size):
    half = (i + 1) // 2
    return lax.rem(size // 2 + jnp.where(lax.rem(i, 2) == 0, half, size - half), size)


def split(value):
    high = value.astype(BF16)
    return high, (value - high.astype(F32)).astype(BF16)


def split3(value):
    high = value.astype(BF16)
    middle, low = split(value - high.astype(F32))
    return high, middle, low


def stack_left(value):
    h, m, l = split3(value)
    return jnp.concatenate([h, h, m, h, m, l], axis=1)


def stack_right(value):
    h, m, l = split3(value)
    return jnp.concatenate([h, m, h, l, m, h], axis=0)


def dot_t(a, b):
    return lax.dot_general(a, b, (((1,), (1,)), ((), ())), preferred_element_type=F32)


def inverse_factor(gram):
    rows = lax.broadcasted_iota(jnp.int32, (RANK, 4 * RANK), 0)
    lanes = lax.broadcasted_iota(jnp.int32, (RANK, 4 * RANK), 1)
    work = jnp.where(lanes == rows + RANK, 1.0, 0.0)
    work = work + jnp.concatenate([gram, jnp.zeros((RANK, 3 * RANK), F32)], axis=1)
    for k in range(RANK):
        row = work[k : k + 1, :]
        pivot = work[k : k + 1, k : k + 1]
        column = work[:, k : k + 1]
        scale = lax.rsqrt(pivot)
        row = row * scale
        step = work - (column * scale) * row
        below = rows > k
        work = jnp.where(below, step, jnp.where(rows == k, row, work))
    return work[:, RANK : 2 * RANK]


def reduce_kernel(
    g_hbm, e_hbm, qt_hbm, merged_out, ag, left_out,
    g_v, e_v, qt_v, high_v, low_v, p_acc, p_loc, p_rs, p_ar, p_all,
    x_src, x_buf, z_src, acc,
    load_sem, p_send, p_recv, x_send, x_recv, z_send, z_recv, ag_send, agf_recv, agx_recv, ag_recv,
):
    dp, mp = lax.axis_index("dp"), lax.axis_index("mp")
    z, x = dp // NX, lax.rem(dp, NX)
    y, core = mp // 2, lax.rem(mp, 2)
    width = g_v.shape[2]
    n_dp = NZ * NX

    def z_peer(i):
        return lax.rem(z + around(i, NZ), NZ)

    def x_peer(i):
        return lax.rem(x + around(i, NX), NX)

    def dp_peer(i):
        return z_peer(i // NX) * NX + x_peer(lax.rem(i, NX))

    def mp_peer(i):
        return lax.rem(y + around(i // 2, NMP // 2), NMP // 2) * 2 + lax.rem(core + i + 1, 2)

    def each(n, act):
        lax.fori_loop(0, n, lambda i, c: (act(i), c)[1], 0)

    def send(src, dst, send_sem, recv_sem, dp_to, mp_to):
        pltpu.make_async_remote_copy(
            src_ref=src, dst_ref=dst, send_sem=send_sem, recv_sem=recv_sem,
            device_id=(dp_to, mp_to), device_id_type=MESH,
        ).start()

    def wait_bytes(ref, sem):
        pltpu.make_async_copy(ref, ref, sem).wait()

    def loads(i):
        cols = pl.ds(pl.multiple_of(i * width, 128), width)
        return (
            pltpu.make_async_copy(qt_hbm.at[:, cols], qt_v.at[i], load_sem.at[2, i]),
            pltpu.make_async_copy(g_hbm.at[0, :, cols], g_v.at[i], load_sem.at[0, i]),
            pltpu.make_async_copy(e_hbm.at[0, :, cols], e_v.at[i], load_sem.at[1, i]),
        )

    for i in range(NX):
        for copy in loads(i):
            copy.start()
        if i == 1:
            barrier = pltpu.get_barrier_semaphore()

            @functools.partial(each, n_dp - 1)
            def _(i):
                pl.semaphore_signal(
                    barrier, inc=1, device_id=(dp_peer(i), mp), device_id_type=MESH
                )

            @functools.partial(each, NMP - 1)
            def _(i):
                pl.semaphore_signal(
                    barrier, inc=1, device_id=(dp, mp_peer(i)), device_id_type=MESH
                )

    drain = []

    p_acc[...] = jnp.zeros_like(p_acc)

    @functools.partial(each, NX)
    def _(i):
        for copy in loads(i):
            copy.wait()
        merged = g_v[i].astype(F32) + e_v[i]
        merged_out[i] = merged
        high, low = split(merged)
        high_v[i] = high
        low_v[i] = low
        q_both = jnp.concatenate(split(qt_v[i]), axis=0)
        p_acc[...] += dot_t(high, q_both) + dot_t(low, q_both)

    p_t = (p_acc[:, :RANK] + p_acc[:, RANK:]).T
    for t in range(NMP):
        p_loc[t] = p_t[8 * (t % 4) : 8 * (t % 4) + 8, 128 * (t // 4) : 128 * (t // 4) + 128]

    pl.semaphore_wait(barrier, n_dp - 1 + NMP - 1)

    @functools.partial(each, NMP - 1)
    def _(i):
        to = mp_peer(i)
        send(p_loc.at[to], p_rs.at[mp], p_send.at[0], p_recv.at[0], dp, to)

    drain.append((p_rs.at[pl.ds(0, NMP - 1)], p_send.at[0]))
    p_rs[mp] = p_loc[mp]
    wait_bytes(p_rs.at[pl.ds(0, NMP - 1)], p_recv.at[0])
    p_ar[dp] = jnp.sum(p_rs[...], axis=0)

    @functools.partial(each, n_dp - 1)
    def _(i):
        send(p_ar.at[dp], p_ar.at[dp], p_send.at[1], p_recv.at[1], dp_peer(i), mp)

    drain.append((p_ar.at[pl.ds(0, n_dp - 1)], p_send.at[1]))
    wait_bytes(p_ar.at[pl.ds(0, n_dp - 1)], p_recv.at[1])
    p_all[mp] = jnp.sum(p_ar[...], axis=0)

    @functools.partial(each, NMP - 1)
    def _(i):
        send(p_all.at[mp], p_all.at[mp], p_send.at[2], p_recv.at[2], dp, mp_peer(i))

    drain.append((p_all.at[pl.ds(0, NMP - 1)], p_send.at[2]))
    wait_bytes(p_all.at[pl.ds(0, NMP - 1)], p_recv.at[2])
    p_t = jnp.concatenate(
        [
            jnp.concatenate([p_all[t] for t in range(4)], axis=0),
            jnp.concatenate([p_all[t] for t in range(4, 8)], axis=0),
        ],
        axis=1,
    )

    p_both = jnp.concatenate(split(p_t), axis=0)
    rows = RANK // NZ

    def compute(to):
        both = jnp.dot(p_both, high_v[to], preferred_element_type=F32)
        both += jnp.dot(p_both, low_v[to], preferred_element_type=F32)
        block = both[:RANK] + both[RANK:]
        for i in range(NZ):
            x_src[to, lax.rem(i - z + NZ, NZ)] = block[i * rows : (i + 1) * rows]

    @functools.partial(each, NX)
    def _(i):
        to = x_peer(i)
        compute(to)

        @pl.when(i < NX - 1)
        def _():
            for f in (0, 2):
                pair = x_src.at[to, pl.ds(2 + f + f // 2, 2)]
                send(pair, x_buf.at[x, pl.ds(f, 2)], x_send, x_recv, z * NX + to, mp)

    drain.append((x_buf.at[pl.ds(0, NX - 1)], x_send))

    def direct(r, slot, n):
        @functools.partial(each, n)
        def _(i):
            to = x_peer(i)
            send(
                x_src.at[to, r], acc.at[slot + x], z_send, z_recv, lax.rem(z + r, NZ) * NX + to, mp
            )

    for d in (1, 0, 2):
        direct(1 + 3 * d, 4 + 4 * d, NX)
    direct(0, 16, NX - 1)
    acc[16 + x] = x_src[x, 0]
    for f in (0, 2):
        x_buf[x, f : f + 2] = x_src[x, 2 + f + f // 2 : 4 + f + f // 2]

    gram = lax.dot_general(
        p_t, p_t, (((1,), (1,)), ((), ())), precision=HIGHEST, preferred_element_type=F32
    )
    inverse = inverse_factor(gram)
    left_out[ROWS:] = stack_left(inverse * (1.0 / n_dp))

    wait_bytes(x_buf.at[pl.ds(0, NX - 1)], x_recv)
    for f in (1, 2, 0, 3):
        z_src[f] = jnp.sum(x_buf[:, f], axis=0)
        to = lax.rem(z + 2 + f + f // 2, NZ)
        send(z_src.at[f], acc.at[f], z_send, z_recv, to * NX + x, mp)

    drain.append((acc.at[pl.ds(0, 19)], z_send))
    p_hat = jnp.dot(inverse, p_t, precision=HIGHEST, preferred_element_type=F32).T
    onto = jnp.dot(p_hat, inverse, precision=HIGHEST, preferred_element_type=F32)
    left_out[:ROWS] = stack_left(onto * (1.0 / n_dp))
    wait_bytes(acc.at[pl.ds(0, 19)], z_recv)
    own = x * NZ + z
    ag[own] = jnp.sum(acc[...], axis=0)

    def spread(piece, r, j, sem):
        to = lax.rem(z + r, NZ) * NX + lax.rem(x + j, NX)
        send(ag.at[piece], ag.at[piece], ag_send, sem, to, mp)

    for j in (2, 1, 3):
        spread(own, 0, j, agx_recv.at[j])
    for f, r in enumerate((3, 5)):
        spread(own, r, 0, agf_recv.at[f])
    for j in (0, 2, 1, 3):
        spread(own, 4, j, ag_recv)
    for r in (2, 6, 1, 7):
        spread(own, r, 0, ag_recv)
    for j in (1, 3, 2):
        piece = lax.rem(x + NX - j, NX) * NZ + z
        wait_bytes(ag.at[piece], agx_recv.at[j])
        for r in (2, 6, 1, 7):
            spread(piece, r, 0, ag_recv)
    for f, r in enumerate((3, 5)):
        piece = x * NZ + lax.rem(z + NZ - r, NZ)
        wait_bytes(ag.at[piece], agf_recv.at[f])
        for j in (2, 1, 3):
            spread(piece, 0, j, ag_recv)

    drain.append((ag.at[pl.ds(0, n_dp - 1)], ag_send))
    wait_bytes(ag.at[pl.ds(0, n_dp - 6)], ag_recv)

    for ref, sem in drain:
        wait_bytes(ref, sem)


def finish_kernel(merged_ref, q_ref, left_ref, u_hbm, n_hbm, q_hbm, u_v, n_v, q_v, sems):
    blocks, _, width = merged_ref.shape
    half = ROWS // 2

    def block(i, carry):
        cols = pl.ds(pl.multiple_of(i * width, 128), width)
        right = stack_right(jnp.concatenate([q_ref[i * NZ + j] for j in range(NZ)], axis=0))
        for h in range(2):
            rows = slice(h * half, (h + 1) * half)
            at = pl.ds(h * half, half)
            recon = jnp.dot(left_ref[rows], right, preferred_element_type=F32)
            n_v[i, rows] = merged_ref[i, rows] - recon
            pltpu.make_async_copy(n_v.at[i, at], n_hbm.at[0, at, cols], sems.at[1]).start()
            u_v[i, rows] = recon.astype(BF16)
            pltpu.make_async_copy(u_v.at[i, at], u_hbm.at[at, cols], sems.at[2]).start()
        q_v[i] = jnp.dot(left_ref[ROWS:], right, preferred_element_type=F32)
        pltpu.make_async_copy(q_v.at[i], q_hbm.at[:, cols], sems.at[0]).start()
        return carry

    lax.fori_loop(0, blocks, block, 0)
    for ref, sem in ((q_v, sems.at[0]), (n_v, sems.at[1]), (u_v, sems.at[2])):
        pltpu.make_async_copy(ref, ref, sem).wait()


def body(grads, errors, q_init):
    columns = grads.shape[2]
    width = columns // NX
    piece = RANK // NZ
    dma = pltpu.SemaphoreType.DMA
    held = pl.pallas_call(
        reduce_kernel,
        out_shape=(
            jax.ShapeDtypeStruct((NX, ROWS, width), F32),
            jax.ShapeDtypeStruct((NX * NZ, piece, width), F32),
            jax.ShapeDtypeStruct((ROWS + RANK, 6 * RANK), BF16),
        ),
        in_specs=[HBM] * 3,
        out_specs=[VMEM] * 3,
        scratch_shapes=[
            pltpu.VMEM((NX, ROWS, width), BF16),
            pltpu.VMEM((NX, ROWS, width), F32),
            pltpu.VMEM((NX, RANK, width), F32),
            pltpu.VMEM((NX, ROWS, width), BF16),
            pltpu.VMEM((NX, ROWS, width), BF16),
            pltpu.VMEM((ROWS, 2 * RANK), F32),
            pltpu.VMEM((NMP, 8, 128), F32),
            pltpu.VMEM((NMP, 8, 128), F32),
            pltpu.VMEM((NZ * NX, 8, 128), F32),
            pltpu.VMEM((NMP, 8, 128), F32),
            pltpu.VMEM((NX, NZ, piece, width), F32),
            pltpu.VMEM((NX, 4, piece, width), F32),
            pltpu.VMEM((4, piece, width), F32),
            pltpu.VMEM((20, piece, width), F32),
            dma((3, NX)),
            dma((3,)),
            dma((3,)),
            dma,
            dma,
            dma,
            dma,
            dma,
            dma((2,)),
            dma((NX,)),
            dma,
        ],
        compiler_params=pltpu.CompilerParams(
            collective_id=0, has_side_effects=True, vmem_limit_bytes=40 << 20
        ),
        name="reduce",
    )(*(pltpu.with_memory_space_constraint(a, pltpu.HBM) for a in (grads, errors, q_init.T)))

    update, new_errors, q_next = pl.pallas_call(
        finish_kernel,
        out_shape=(
            jax.ShapeDtypeStruct((ROWS, columns), BF16),
            jax.ShapeDtypeStruct((1, ROWS, columns), F32),
            jax.ShapeDtypeStruct((RANK, columns), F32),
        ),
        in_specs=[VMEM] * 3,
        out_specs=[HBM] * 3,
        scratch_shapes=[
            pltpu.VMEM((NX, ROWS, width), BF16),
            pltpu.VMEM((NX, ROWS, width), F32),
            pltpu.VMEM((NX, RANK, width), F32),
            dma((3,)),
        ],
        compiler_params=pltpu.CompilerParams(vmem_limit_bytes=32 << 20),
        name="finish",
    )(*held)
    return (update, new_errors, q_next.T)


def solution(mesh):
    placed = (P("dp", None, "mp"), P("dp", None, "mp"), P("mp", None))
    return jax.shard_map(
        body,
        mesh=mesh,
        in_specs=placed,
        out_specs=(P(None, "mp"), P("dp", None, "mp"), P("mp", None)),
        check_vma=False,
    )
```

```python
import functools

import jax
import jax.numpy as jnp
from jax import lax
from jax.experimental import pallas as pl
from jax.experimental.pallas import tpu as pltpu
from jax.sharding import PartitionSpec as P

MESH = pl.DeviceIdType.MESH
HIGHEST = lax.Precision.HIGHEST
F32 = jnp.float32
BF16 = jnp.bfloat16

NZ, NX, NMP = 8, 4, 8
ROWS, RANK = 256, 32
VMEM = pl.BlockSpec(memory_space=pltpu.VMEM)
HBM = pl.BlockSpec(memory_space=pltpu.HBM)


def around(i, size):
    half = (i + 1) // 2
    return lax.rem(size // 2 + jnp.where(lax.rem(i, 2) == 0, half, size - half), size)


def split(value):
    high = value.astype(BF16)
    return high, (value - high.astype(F32)).astype(BF16)


def split3(value):
    high = value.astype(BF16)
    middle, low = split(value - high.astype(F32))
    return high, middle, low


def stack_left(value):
    h, m, l = split3(value)
    return jnp.concatenate([h, h, m, h, m, l], axis=1)


def stack_right(value):
    h, m, l = split3(value)
    return jnp.concatenate([h, m, h, l, m, h], axis=0)


def dot_t(a, b):
    return lax.dot_general(a, b, (((1,), (1,)), ((), ())), preferred_element_type=F32)


def inverse_factor(gram):
    rows = lax.broadcasted_iota(jnp.int32, (RANK, 4 * RANK), 0)
    lanes = lax.broadcasted_iota(jnp.int32, (RANK, 4 * RANK), 1)
    work = jnp.where(lanes == rows + RANK, 1.0, 0.0)
    work = work + jnp.concatenate([gram, jnp.zeros((RANK, 3 * RANK), F32)], axis=1)
    for k in range(RANK):
        row = work[k : k + 1, :]
        pivot = work[k : k + 1, k : k + 1]
        column = work[:, k : k + 1]
        scale = lax.rsqrt(pivot)
        row = row * scale
        step = work - (column * scale) * row
        below = rows > k
        work = jnp.where(below, step, jnp.where(rows == k, row, work))
    return work[:, RANK : 2 * RANK]


def reduce_kernel(
    g_hbm, e_hbm, qt_hbm, merged_out, ag, left_out,
    g_v, e_v, qt_v, high_v, low_v, p_acc, p_loc, p_rs, p_ar, p_all,
    x_src, x_buf, z_src, acc,
    load_sem, p_send, p_recv, x_send, x_recv, z_send, z_recv, ag_send, agf_recv, agx_recv, ag_recv,
):
    dp, mp = lax.axis_index("dp"), lax.axis_index("mp")
    z, x = dp // NX, lax.rem(dp, NX)
    y, core = mp // 2, lax.rem(mp, 2)
    width = g_v.shape[2]
    n_dp = NZ * NX

    def z_peer(i):
        return lax.rem(z + around(i, NZ), NZ)

    def x_peer(i):
        return lax.rem(x + around(i, NX), NX)

    def dp_peer(i):
        return z_peer(i // NX) * NX + x_peer(lax.rem(i, NX))

    def y_peer(i):
        return lax.rem(y + around(i, NMP // 2), NMP // 2)

    def each(n, act):
        lax.fori_loop(0, n, lambda i, c: (act(i), c)[1], 0)

    def send(src, dst, send_sem, recv_sem, dp_to, mp_to):
        pltpu.make_async_remote_copy(
            src_ref=src, dst_ref=dst, send_sem=send_sem, recv_sem=recv_sem,
            device_id=(dp_to, mp_to), device_id_type=MESH,
        ).start()

    def wait_bytes(ref, sem):
        pltpu.make_async_copy(ref, ref, sem).wait()

    def loads(i):
        cols = pl.ds(pl.multiple_of(i * width, 128), width)
        return (
            pltpu.make_async_copy(qt_hbm.at[:, cols], qt_v.at[i], load_sem.at[2, i]),
            pltpu.make_async_copy(g_hbm.at[0, :, cols], g_v.at[i], load_sem.at[0, i]),
            pltpu.make_async_copy(e_hbm.at[0, :, cols], e_v.at[i], load_sem.at[1, i]),
        )

    for i in range(NX):
        for copy in loads(i):
            copy.start()
        if i == 1:
            barrier = pltpu.get_barrier_semaphore()

            @pl.when(core == 1)
            def _():
                @functools.partial(each, n_dp - 1)
                def _(i):
                    pl.semaphore_signal(
                        barrier, inc=1, device_id=(dp_peer(i), mp), device_id_type=MESH
                    )

                @functools.partial(each, NMP // 2)
                def _(i):
                    pl.semaphore_signal(
                        barrier, inc=1, device_id=(dp, y_peer(i) * 2), device_id_type=MESH
                    )

                @functools.partial(each, NMP // 2 - 1)
                def _(i):
                    pl.semaphore_signal(
                        barrier, inc=1, device_id=(dp, y_peer(i) * 2 + 1), device_id_type=MESH
                    )

            @pl.when(core == 0)
            def _():
                @functools.partial(each, NMP // 2)
                def _(i):
                    pl.semaphore_signal(
                        barrier, inc=1, device_id=(dp, y_peer(i) * 2 + 1), device_id_type=MESH
                    )

    drain = []

    p_acc[...] = jnp.zeros_like(p_acc)

    @functools.partial(each, NX)
    def _(i):
        for copy in loads(i):
            copy.wait()
        merged = g_v[i].astype(F32) + e_v[i]
        merged_out[i] = merged
        high, low = split(merged)
        high_v[i] = high
        low_v[i] = low
        q_both = jnp.concatenate(split(qt_v[i]), axis=0)
        p_acc[...] += dot_t(high, q_both) + dot_t(low, q_both)

    p_t = (p_acc[:, :RANK] + p_acc[:, RANK:]).T
    for t in range(NMP // 2):
        p_loc[t] = p_t[16 * (t % 2) : 16 * (t % 2) + 16, 128 * (t // 2) : 128 * (t // 2) + 128]

    @pl.when(core == 1)
    def _():
        pl.semaphore_wait(barrier, n_dp - 1 + NMP - 1)

    @pl.when(core == 0)
    def _():
        pl.semaphore_wait(barrier, NMP // 2)

    ys = NMP // 2

    def scatter(i):
        to = y_peer(i)
        send(p_loc.at[to], p_rs.at[mp], p_send.at[0], p_recv.at[0], dp, to * 2 + 1)

    def gather(i, c):
        send(p_all.at[y], p_all.at[y], p_send.at[2], p_recv.at[2], dp, y_peer(i) * 2 + c)

    @pl.when(core == 0)
    def _():
        each(ys, scatter)
        wait_bytes(p_all.at[pl.ds(0, ys)], p_recv.at[2])

    @pl.when(core == 1)
    def _():
        each(ys - 1, scatter)
        p_rs[mp] = p_loc[y]
        wait_bytes(p_rs.at[pl.ds(0, NMP - 1)], p_recv.at[0])
        p_ar[dp] = jnp.sum(p_rs[...], axis=0)

        @functools.partial(each, n_dp - 1)
        def _(i):
            send(p_ar.at[dp], p_ar.at[dp], p_send.at[1], p_recv.at[1], dp_peer(i), mp)

        wait_bytes(p_ar.at[pl.ds(0, n_dp - 1)], p_recv.at[1])
        p_all[y] = jnp.sum(p_ar[...], axis=0)
        each(ys, lambda i: gather(i, 0))
        each(ys - 1, lambda i: gather(i, 1))
        wait_bytes(p_all.at[pl.ds(0, ys - 1)], p_recv.at[2])

    p_t = jnp.concatenate(
        [
            jnp.concatenate([p_all[0], p_all[1]], axis=0),
            jnp.concatenate([p_all[2], p_all[3]], axis=0),
        ],
        axis=1,
    )

    p_both = jnp.concatenate(split(p_t), axis=0)
    rows = RANK // NZ

    def compute(to):
        both = jnp.dot(p_both, high_v[to], preferred_element_type=F32)
        both += jnp.dot(p_both, low_v[to], preferred_element_type=F32)
        block = both[:RANK] + both[RANK:]
        for i in range(NZ):
            x_src[to, lax.rem(i - z + NZ, NZ)] = block[i * rows : (i + 1) * rows]

    @functools.partial(each, NX)
    def _(i):
        to = x_peer(i)
        compute(to)

        @pl.when(i < NX - 1)
        def _():
            for f in (0, 2):
                pair = x_src.at[to, pl.ds(2 + f + f // 2, 2)]
                send(pair, x_buf.at[x, pl.ds(f, 2)], x_send, x_recv, z * NX + to, mp)

    drain.append((x_buf.at[pl.ds(0, NX - 1)], x_send))

    def direct(r, slot, n):
        @functools.partial(each, n)
        def _(i):
            to = x_peer(i)
            send(
                x_src.at[to, r], acc.at[slot + x], z_send, z_recv, lax.rem(z + r, NZ) * NX + to, mp
            )

    for d in (1, 0, 2):
        direct(1 + 3 * d, 4 + 4 * d, NX)
    direct(0, 16, NX - 1)
    acc[16 + x] = x_src[x, 0]
    for f in (0, 2):
        x_buf[x, f : f + 2] = x_src[x, 2 + f + f // 2 : 4 + f + f // 2]

    gram = lax.dot_general(
        p_t, p_t, (((1,), (1,)), ((), ())), precision=HIGHEST, preferred_element_type=F32
    )
    inverse = inverse_factor(gram)
    left_out[ROWS:] = stack_left(inverse * (1.0 / n_dp))

    wait_bytes(x_buf.at[pl.ds(0, NX - 1)], x_recv)
    for f in (1, 2, 0, 3):
        z_src[f] = jnp.sum(x_buf[:, f], axis=0)
        to = lax.rem(z + 2 + f + f // 2, NZ)
        send(z_src.at[f], acc.at[f], z_send, z_recv, to * NX + x, mp)

    drain.append((acc.at[pl.ds(0, 19)], z_send))
    p_hat = jnp.dot(inverse, p_t, precision=HIGHEST, preferred_element_type=F32).T
    onto = jnp.dot(p_hat, inverse, precision=HIGHEST, preferred_element_type=F32)
    left_out[:ROWS] = stack_left(onto * (1.0 / n_dp))
    wait_bytes(acc.at[pl.ds(0, 19)], z_recv)
    own = x * NZ + z
    ag[own] = jnp.sum(acc[...], axis=0)

    def spread(piece, r, j, sem):
        to = lax.rem(z + r, NZ) * NX + lax.rem(x + j, NX)
        send(ag.at[piece], ag.at[piece], ag_send, sem, to, mp)

    for j in (2, 1, 3):
        spread(own, 0, j, agx_recv.at[j])
    for f, r in enumerate((3, 5)):
        spread(own, r, 0, agf_recv.at[f])
    for j in (0, 2, 1, 3):
        spread(own, 4, j, ag_recv)
    for r in (2, 6, 1, 7):
        spread(own, r, 0, ag_recv)
    for j in (1, 3, 2):
        piece = lax.rem(x + NX - j, NX) * NZ + z
        wait_bytes(ag.at[piece], agx_recv.at[j])
        for r in (2, 6, 1, 7):
            spread(piece, r, 0, ag_recv)
    for f, r in enumerate((3, 5)):
        piece = x * NZ + lax.rem(z + NZ - r, NZ)
        wait_bytes(ag.at[piece], agf_recv.at[f])
        for j in (2, 1, 3):
            spread(piece, 0, j, ag_recv)

    drain.append((ag.at[pl.ds(0, n_dp - 1)], ag_send))
    wait_bytes(ag.at[pl.ds(0, n_dp - 6)], ag_recv)

    for ref, sem in drain:
        wait_bytes(ref, sem)

    @pl.when(core == 0)
    def _():
        wait_bytes(p_rs.at[pl.ds(0, ys)], p_send.at[0])

    @pl.when(core == 1)
    def _():
        wait_bytes(p_rs.at[pl.ds(0, ys - 1)], p_send.at[0])
        wait_bytes(p_ar.at[pl.ds(0, n_dp - 1)], p_send.at[1])
        wait_bytes(p_rs.at[pl.ds(0, NMP - 1)], p_send.at[2])


def finish_kernel(merged_ref, q_ref, left_ref, u_hbm, n_hbm, q_hbm, u_v, n_v, q_v, sems):
    blocks, _, width = merged_ref.shape
    half = ROWS // 2

    def block(i, carry):
        cols = pl.ds(pl.multiple_of(i * width, 128), width)
        right = stack_right(jnp.concatenate([q_ref[i * NZ + j] for j in range(NZ)], axis=0))
        for h in range(2):
            rows = slice(h * half, (h + 1) * half)
            at = pl.ds(h * half, half)
            recon = jnp.dot(left_ref[rows], right, preferred_element_type=F32)
            n_v[i, rows] = merged_ref[i, rows] - recon
            pltpu.make_async_copy(n_v.at[i, at], n_hbm.at[0, at, cols], sems.at[1]).start()
            u_v[i, rows] = recon.astype(BF16)
            pltpu.make_async_copy(u_v.at[i, at], u_hbm.at[at, cols], sems.at[2]).start()
        q_v[i] = jnp.dot(left_ref[ROWS:], right, preferred_element_type=F32)
        pltpu.make_async_copy(q_v.at[i], q_hbm.at[:, cols], sems.at[0]).start()
        return carry

    lax.fori_loop(0, blocks, block, 0)
    for ref, sem in ((q_v, sems.at[0]), (n_v, sems.at[1]), (u_v, sems.at[2])):
        pltpu.make_async_copy(ref, ref, sem).wait()


def body(grads, errors, q_init):
    columns = grads.shape[2]
    width = columns // NX
    piece = RANK // NZ
    dma = pltpu.SemaphoreType.DMA
    held = pl.pallas_call(
        reduce_kernel,
        out_shape=(
            jax.ShapeDtypeStruct((NX, ROWS, width), F32),
            jax.ShapeDtypeStruct((NX * NZ, piece, width), F32),
            jax.ShapeDtypeStruct((ROWS + RANK, 6 * RANK), BF16),
        ),
        in_specs=[HBM] * 3,
        out_specs=[VMEM] * 3,
        scratch_shapes=[
            pltpu.VMEM((NX, ROWS, width), BF16),
            pltpu.VMEM((NX, ROWS, width), F32),
            pltpu.VMEM((NX, RANK, width), F32),
            pltpu.VMEM((NX, ROWS, width), BF16),
            pltpu.VMEM((NX, ROWS, width), BF16),
            pltpu.VMEM((ROWS, 2 * RANK), F32),
            pltpu.VMEM((NMP // 2, 16, 128), F32),
            pltpu.VMEM((NMP, 16, 128), F32),
            pltpu.VMEM((NZ * NX, 16, 128), F32),
            pltpu.VMEM((NMP // 2, 16, 128), F32),
            pltpu.VMEM((NX, NZ, piece, width), F32),
            pltpu.VMEM((NX, 4, piece, width), F32),
            pltpu.VMEM((4, piece, width), F32),
            pltpu.VMEM((20, piece, width), F32),
            dma((3, NX)),
            dma((3,)),
            dma((3,)),
            dma,
            dma,
            dma,
            dma,
            dma,
            dma((2,)),
            dma((NX,)),
            dma,
        ],
        compiler_params=pltpu.CompilerParams(
            collective_id=0, has_side_effects=True, vmem_limit_bytes=40 << 20
        ),
        name="reduce",
    )(*(pltpu.with_memory_space_constraint(a, pltpu.HBM) for a in (grads, errors, q_init.T)))

    update, new_errors, q_next = pl.pallas_call(
        finish_kernel,
        out_shape=(
            jax.ShapeDtypeStruct((ROWS, columns), BF16),
            jax.ShapeDtypeStruct((1, ROWS, columns), F32),
            jax.ShapeDtypeStruct((RANK, columns), F32),
        ),
        in_specs=[VMEM] * 3,
        out_specs=[HBM] * 3,
        scratch_shapes=[
            pltpu.VMEM((NX, ROWS, width), BF16),
            pltpu.VMEM((NX, ROWS, width), F32),
            pltpu.VMEM((NX, RANK, width), F32),
            dma((3,)),
        ],
        compiler_params=pltpu.CompilerParams(vmem_limit_bytes=32 << 20),
        name="finish",
    )(*held)
    return (update, new_errors, q_next.T)


def solution(mesh):
    placed = (P("dp", None, "mp"), P("dp", None, "mp"), P("mp", None))
    return jax.shard_map(
        body,
        mesh=mesh,
        in_specs=placed,
        out_specs=(P(None, "mp"), P("dp", None, "mp"), P("mp", None)),
        check_vma=False,
    )
```

```python
import functools

import jax
import jax.numpy as jnp
from jax import lax
from jax.experimental import pallas as pl
from jax.experimental.pallas import tpu as pltpu
from jax.sharding import PartitionSpec as P

MESH = pl.DeviceIdType.MESH
HIGHEST = lax.Precision.HIGHEST
F32 = jnp.float32
BF16 = jnp.bfloat16

NZ, NX, NMP = 8, 4, 8
ROWS, RANK = 256, 32
VMEM = pl.BlockSpec(memory_space=pltpu.VMEM)
HBM = pl.BlockSpec(memory_space=pltpu.HBM)


def around(i, size):
    half = (i + 1) // 2
    return lax.rem(size // 2 + jnp.where(lax.rem(i, 2) == 0, half, size - half), size)


def split(value):
    high = value.astype(BF16)
    return high, (value - high.astype(F32)).astype(BF16)


def split3(value):
    high = value.astype(BF16)
    middle, low = split(value - high.astype(F32))
    return high, middle, low


def stack_left(value):
    h, m, l = split3(value)
    return jnp.concatenate([h, h, m, h, m, l], axis=1)


def stack_right(value):
    h, m, l = split3(value)
    return jnp.concatenate([h, m, h, l, m, h], axis=0)


def dot_t(a, b):
    return lax.dot_general(a, b, (((1,), (1,)), ((), ())), preferred_element_type=F32)


def inverse_factor(gram):
    rows = lax.broadcasted_iota(jnp.int32, (RANK, 4 * RANK), 0)
    lanes = lax.broadcasted_iota(jnp.int32, (RANK, 4 * RANK), 1)
    work = jnp.where(lanes == rows + RANK, 1.0, 0.0)
    work = work + jnp.concatenate([gram, jnp.zeros((RANK, 3 * RANK), F32)], axis=1)
    for k in range(RANK):
        row = work[k : k + 1, :]
        pivot = work[k : k + 1, k : k + 1]
        column = work[:, k : k + 1]
        scale = lax.rsqrt(pivot)
        row = row * scale
        step = work - (column * scale) * row
        below = rows > k
        work = jnp.where(below, step, jnp.where(rows == k, row, work))
    return work[:, RANK : 2 * RANK]


def reduce_kernel(
    g_hbm, e_hbm, qt_hbm, merged_out, ag, left_out,
    g_v, e_v, qt_v, high_v, low_v, p_acc, p_loc, p_rs, p_ar, p_all,
    x_src, x_buf, z_src, acc, aux, inv_v,
    load_sem, p_send, p_recv, x_send, x_recv, z_send, z_recv, ag_send, agf_recv, agx_recv, ag_recv, aux_recv, inv_sem,
):
    dp, mp = lax.axis_index("dp"), lax.axis_index("mp")
    z, x = dp // NX, lax.rem(dp, NX)
    y, core = mp // 2, lax.rem(mp, 2)
    width = g_v.shape[2]
    n_dp = NZ * NX

    def z_peer(i):
        return lax.rem(z + around(i, NZ), NZ)

    def x_peer(i):
        return lax.rem(x + around(i, NX), NX)

    def dp_peer(i):
        return z_peer(i // NX) * NX + x_peer(lax.rem(i, NX))

    def y_peer(i):
        return lax.rem(y + around(i, NMP // 2), NMP // 2)

    def each(n, act):
        lax.fori_loop(0, n, lambda i, c: (act(i), c)[1], 0)

    def send(src, dst, send_sem, recv_sem, dp_to, mp_to):
        pltpu.make_async_remote_copy(
            src_ref=src, dst_ref=dst, send_sem=send_sem, recv_sem=recv_sem,
            device_id=(dp_to, mp_to), device_id_type=MESH,
        ).start()

    def wait_bytes(ref, sem):
        pltpu.make_async_copy(ref, ref, sem).wait()

    def loads(i):
        cols = pl.ds(pl.multiple_of(i * width, 128), width)
        return (
            pltpu.make_async_copy(qt_hbm.at[:, cols], qt_v.at[i], load_sem.at[2, i]),
            pltpu.make_async_copy(g_hbm.at[0, :, cols], g_v.at[i], load_sem.at[0, i]),
            pltpu.make_async_copy(e_hbm.at[0, :, cols], e_v.at[i], load_sem.at[1, i]),
        )

    for i in range(NX):
        for copy in loads(i):
            copy.start()
        if i == 1:
            barrier = pltpu.get_barrier_semaphore()

            @pl.when(core == 1)
            def _():
                @functools.partial(each, n_dp - 1)
                def _(i):
                    pl.semaphore_signal(
                        barrier, inc=1, device_id=(dp_peer(i), mp), device_id_type=MESH
                    )

                @functools.partial(each, NMP // 2)
                def _(i):
                    pl.semaphore_signal(
                        barrier, inc=1, device_id=(dp, y_peer(i) * 2), device_id_type=MESH
                    )

                @functools.partial(each, NMP // 2 - 1)
                def _(i):
                    pl.semaphore_signal(
                        barrier, inc=1, device_id=(dp, y_peer(i) * 2 + 1), device_id_type=MESH
                    )

            @pl.when(core == 0)
            def _():
                @functools.partial(each, NMP // 2)
                def _(i):
                    pl.semaphore_signal(
                        barrier, inc=1, device_id=(dp, y_peer(i) * 2 + 1), device_id_type=MESH
                    )

    drain = []

    p_acc[...] = jnp.zeros_like(p_acc)

    @functools.partial(each, NX)
    def _(i):
        for copy in loads(i):
            copy.wait()
        merged = g_v[i].astype(F32) + e_v[i]
        merged_out[i] = merged
        high, low = split(merged)
        high_v[i] = high
        low_v[i] = low
        q_both = jnp.concatenate(split(qt_v[i]), axis=0)
        p_acc[...] += dot_t(high, q_both) + dot_t(low, q_both)

    p_t = (p_acc[:, :RANK] + p_acc[:, RANK:]).T
    for t in range(NMP // 2):
        p_loc[t] = p_t[16 * (t % 2) : 16 * (t % 2) + 16, 128 * (t // 2) : 128 * (t // 2) + 128]

    @pl.when(core == 1)
    def _():
        pl.semaphore_wait(barrier, n_dp - 1 + NMP - 1)

    @pl.when(core == 0)
    def _():
        pl.semaphore_wait(barrier, NMP // 2)

    ys = NMP // 2

    def scatter(i):
        to = y_peer(i)
        send(p_loc.at[to], p_rs.at[mp], p_send.at[0], p_recv.at[0], dp, to * 2 + 1)

    def gather(i, c):
        send(p_all.at[y], p_all.at[y], p_send.at[2], p_recv.at[2], dp, y_peer(i) * 2 + c)

    @pl.when(core == 0)
    def _():
        each(ys, scatter)
        wait_bytes(p_all.at[pl.ds(0, ys)], p_recv.at[2])

    @pl.when(core == 1)
    def _():
        each(ys - 1, scatter)
        p_rs[mp] = p_loc[y]
        wait_bytes(p_rs.at[pl.ds(0, NMP - 1)], p_recv.at[0])
        p_ar[dp] = jnp.sum(p_rs[...], axis=0)

        @functools.partial(each, n_dp - 1)
        def _(i):
            send(p_ar.at[dp], p_ar.at[dp], p_send.at[1], p_recv.at[1], dp_peer(i), mp)

        wait_bytes(p_ar.at[pl.ds(0, n_dp - 1)], p_recv.at[1])
        p_all[y] = jnp.sum(p_ar[...], axis=0)
        each(ys, lambda i: gather(i, 0))
        each(ys - 1, lambda i: gather(i, 1))
        wait_bytes(p_all.at[pl.ds(0, ys - 1)], p_recv.at[2])

    p_t = jnp.concatenate(
        [
            jnp.concatenate([p_all[0], p_all[1]], axis=0),
            jnp.concatenate([p_all[2], p_all[3]], axis=0),
        ],
        axis=1,
    )

    p_both = jnp.concatenate(split(p_t), axis=0)
    rows = RANK // NZ

    def compute(to):
        both = jnp.dot(p_both, high_v[to], preferred_element_type=F32)
        both += jnp.dot(p_both, low_v[to], preferred_element_type=F32)
        block = both[:RANK] + both[RANK:]
        for i in range(NZ):
            x_src[to, lax.rem(i - z + NZ, NZ)] = block[i * rows : (i + 1) * rows]

    @functools.partial(each, NX)
    def _(i):
        to = x_peer(i)
        compute(to)

        @pl.when(i < NX - 1)
        def _():
            for f in (0, 2):
                pair = x_src.at[to, pl.ds(2 + f + f // 2, 2)]
                send(pair, x_buf.at[x, pl.ds(f, 2)], x_send, x_recv, z * NX + to, mp)

    drain.append((x_buf.at[pl.ds(0, NX - 1)], x_send))

    def direct(r, slot, n):
        @functools.partial(each, n)
        def _(i):
            to = x_peer(i)
            send(
                x_src.at[to, r], acc.at[slot + x], z_send, z_recv, lax.rem(z + r, NZ) * NX + to, mp
            )

    for d in (1, 0, 2):
        direct(1 + 3 * d, 4 + 4 * d, NX)
    direct(0, 16, NX - 1)
    acc[16 + x] = x_src[x, 0]
    for f in (0, 2):
        x_buf[x, f : f + 2] = x_src[x, 2 + f + f // 2 : 4 + f + f // 2]

    def factor():
        gram = lax.dot_general(
            p_t, p_t, (((1,), (1,)), ((), ())), precision=HIGHEST, preferred_element_type=F32
        )
        inverse = inverse_factor(gram)
        return inverse

    def project(inverse):
        left_out[ROWS:] = stack_left(inverse * (1.0 / n_dp))
        p_hat = jnp.dot(inverse, p_t, precision=HIGHEST, preferred_element_type=F32).T
        onto = jnp.dot(p_hat, inverse, precision=HIGHEST, preferred_element_type=F32)
        left_out[:ROWS] = stack_left(onto * (1.0 / n_dp))

    wait_bytes(x_buf.at[pl.ds(0, NX - 1)], x_recv)
    for f in (1, 2, 0, 3):
        z_src[f] = jnp.sum(x_buf[:, f], axis=0)
        to = lax.rem(z + 2 + f + f // 2, NZ)
        send(z_src.at[f], acc.at[f], z_send, z_recv, to * NX + x, mp)

    drain.append((acc.at[pl.ds(0, 19)], z_send))
    wait_bytes(acc.at[pl.ds(0, 19)], z_recv)
    own = x * NZ + z
    ag[own] = jnp.sum(acc[...], axis=0)

    near, far = (2, 6, 1, 7), (3, 5)

    def spread(src, piece, r, j, c, sem):
        to = lax.rem(z + r, NZ) * NX + lax.rem(x + j, NX)
        send(src, ag.at[piece], ag_send, sem, to, y * 2 + c)

    @pl.when(core == 0)
    def _():
        for j in (2, 1, 3):
            to = z * NX + lax.rem(x + j, NX)
            send(ag.at[own], aux.at[j - 1], ag_send, aux_recv.at[j - 1], to, mp + 1)
        for f, r in enumerate(far):
            to = lax.rem(z + r, NZ) * NX + x
            send(ag.at[own], aux.at[3 + f], ag_send, aux_recv.at[3 + f], to, mp + 1)
        for j in (0, 2, 1, 3):
            spread(ag.at[own], own, 4, j, 0, ag_recv)
        for r in near:
            spread(ag.at[own], own, r, 0, 0, ag_recv)
        inverse = factor()
        inv_v[...] = jnp.concatenate([inverse, jnp.zeros((RANK, 3 * RANK), F32)], axis=1)
        send(inv_v, inv_v, inv_sem.at[0], inv_sem.at[1], dp, mp + 1)
        project(inverse)
        wait_bytes(ag.at[pl.ds(0, n_dp - 1)], ag_recv)
        wait_bytes(ag.at[pl.ds(0, 13)], ag_send)
        wait_bytes(inv_v, inv_sem.at[0])

    @pl.when(core == 1)
    def _():
        for j in (2, 1, 3):
            spread(ag.at[own], own, 0, j, 1, agx_recv.at[j])
        for f, r in enumerate(far):
            spread(ag.at[own], own, r, 0, 1, agf_recv.at[f])
        for j in (0, 2, 1, 3):
            spread(ag.at[own], own, 4, j, 1, ag_recv)
        for r in near:
            spread(ag.at[own], own, r, 0, 1, ag_recv)
        for j in (1, 3, 2):
            piece = lax.rem(x + NX - j, NX) * NZ + z
            wait_bytes(ag.at[piece], agx_recv.at[j])
            for r in near:
                spread(ag.at[piece], piece, r, 0, 1, ag_recv)
        for f, r in enumerate(far):
            piece = x * NZ + lax.rem(z + NZ - r, NZ)
            wait_bytes(ag.at[piece], agf_recv.at[f])
            for j in (2, 1, 3):
                spread(ag.at[piece], piece, 0, j, 1, ag_recv)
        for j in (1, 3, 2):
            piece = lax.rem(x + NX - j, NX) * NZ + z
            wait_bytes(aux.at[j - 1], aux_recv.at[j - 1])
            for r in near + (0,):
                spread(aux.at[j - 1], piece, r, 0, 0, ag_recv)
        for f, r in enumerate(far):
            piece = x * NZ + lax.rem(z + NZ - r, NZ)
            wait_bytes(aux.at[3 + f], aux_recv.at[3 + f])
            for j in (2, 1, 3, 0):
                spread(aux.at[3 + f], piece, 0, j, 0, ag_recv)
        wait_bytes(inv_v, inv_sem.at[1])
        project(inv_v[:, :RANK])
        wait_bytes(ag.at[pl.ds(0, n_dp - 6)], ag_recv)
        wait_bytes(ag.at[pl.ds(0, n_dp - 1)], ag_send)
        wait_bytes(ag.at[pl.ds(0, 23)], ag_send)

    for ref, sem in drain:
        wait_bytes(ref, sem)

    @pl.when(core == 0)
    def _():
        wait_bytes(p_rs.at[pl.ds(0, ys)], p_send.at[0])

    @pl.when(core == 1)
    def _():
        wait_bytes(p_rs.at[pl.ds(0, ys - 1)], p_send.at[0])
        wait_bytes(p_ar.at[pl.ds(0, n_dp - 1)], p_send.at[1])
        wait_bytes(p_rs.at[pl.ds(0, NMP - 1)], p_send.at[2])


def finish_kernel(merged_ref, q_ref, left_ref, u_hbm, n_hbm, q_hbm, u_v, n_v, q_v, sems):
    blocks, _, width = merged_ref.shape
    half = ROWS // 2

    def block(i, carry):
        cols = pl.ds(pl.multiple_of(i * width, 128), width)
        right = stack_right(jnp.concatenate([q_ref[i * NZ + j] for j in range(NZ)], axis=0))
        for h in range(2):
            rows = slice(h * half, (h + 1) * half)
            at = pl.ds(h * half, half)
            recon = jnp.dot(left_ref[rows], right, preferred_element_type=F32)
            n_v[i, rows] = merged_ref[i, rows] - recon
            pltpu.make_async_copy(n_v.at[i, at], n_hbm.at[0, at, cols], sems.at[1]).start()
            u_v[i, rows] = recon.astype(BF16)
            pltpu.make_async_copy(u_v.at[i, at], u_hbm.at[at, cols], sems.at[2]).start()
        q_v[i] = jnp.dot(left_ref[ROWS:], right, preferred_element_type=F32)
        pltpu.make_async_copy(q_v.at[i], q_hbm.at[:, cols], sems.at[0]).start()
        return carry

    lax.fori_loop(0, blocks, block, 0)
    for ref, sem in ((q_v, sems.at[0]), (n_v, sems.at[1]), (u_v, sems.at[2])):
        pltpu.make_async_copy(ref, ref, sem).wait()


def body(grads, errors, q_init):
    columns = grads.shape[2]
    width = columns // NX
    piece = RANK // NZ
    dma = pltpu.SemaphoreType.DMA
    held = pl.pallas_call(
        reduce_kernel,
        out_shape=(
            jax.ShapeDtypeStruct((NX, ROWS, width), F32),
            jax.ShapeDtypeStruct((NX * NZ, piece, width), F32),
            jax.ShapeDtypeStruct((ROWS + RANK, 6 * RANK), BF16),
        ),
        in_specs=[HBM] * 3,
        out_specs=[VMEM] * 3,
        scratch_shapes=[
            pltpu.VMEM((NX, ROWS, width), BF16),
            pltpu.VMEM((NX, ROWS, width), F32),
            pltpu.VMEM((NX, RANK, width), F32),
            pltpu.VMEM((NX, ROWS, width), BF16),
            pltpu.VMEM((NX, ROWS, width), BF16),
            pltpu.VMEM((ROWS, 2 * RANK), F32),
            pltpu.VMEM((NMP // 2, 16, 128), F32),
            pltpu.VMEM((NMP, 16, 128), F32),
            pltpu.VMEM((NZ * NX, 16, 128), F32),
            pltpu.VMEM((NMP // 2, 16, 128), F32),
            pltpu.VMEM((NX, NZ, piece, width), F32),
            pltpu.VMEM((NX, 4, piece, width), F32),
            pltpu.VMEM((4, piece, width), F32),
            pltpu.VMEM((20, piece, width), F32),
            pltpu.VMEM((5, piece, width), F32),
            pltpu.VMEM((RANK, 4 * RANK), F32),
            dma((3, NX)),
            dma((3,)),
            dma((3,)),
            dma,
            dma,
            dma,
            dma,
            dma,
            dma((2,)),
            dma((NX,)),
            dma,
            dma((5,)),
            dma((2,)),
        ],
        compiler_params=pltpu.CompilerParams(
            collective_id=0, has_side_effects=True, vmem_limit_bytes=40 << 20
        ),
        name="reduce",
    )(*(pltpu.with_memory_space_constraint(a, pltpu.HBM) for a in (grads, errors, q_init.T)))

    update, new_errors, q_next = pl.pallas_call(
        finish_kernel,
        out_shape=(
            jax.ShapeDtypeStruct((ROWS, columns), BF16),
            jax.ShapeDtypeStruct((1, ROWS, columns), F32),
            jax.ShapeDtypeStruct((RANK, columns), F32),
        ),
        in_specs=[VMEM] * 3,
        out_specs=[HBM] * 3,
        scratch_shapes=[
            pltpu.VMEM((NX, ROWS, width), BF16),
            pltpu.VMEM((NX, ROWS, width), F32),
            pltpu.VMEM((NX, RANK, width), F32),
            dma((3,)),
        ],
        compiler_params=pltpu.CompilerParams(vmem_limit_bytes=32 << 20),
        name="finish",
    )(*held)
    return (update, new_errors, q_next.T)


def solution(mesh):
    placed = (P("dp", None, "mp"), P("dp", None, "mp"), P("mp", None))
    return jax.shard_map(
        body,
        mesh=mesh,
        in_specs=placed,
        out_specs=(P(None, "mp"), P("dp", None, "mp"), P("mp", None)),
        check_vma=False,
    )
```

```python
import functools

import jax
import jax.numpy as jnp
from jax import lax
from jax.experimental import pallas as pl
from jax.experimental.pallas import tpu as pltpu
from jax.sharding import PartitionSpec as P

MESH = pl.DeviceIdType.MESH
HIGHEST = lax.Precision.HIGHEST
F32 = jnp.float32
BF16 = jnp.bfloat16

NZ, NX, NMP = 8, 4, 8
ROWS, RANK = 256, 32
VMEM = pl.BlockSpec(memory_space=pltpu.VMEM)
HBM = pl.BlockSpec(memory_space=pltpu.HBM)


def around(i, size):
    half = (i + 1) // 2
    return lax.rem(size // 2 + jnp.where(lax.rem(i, 2) == 0, half, size - half), size)


def split(value):
    high = value.astype(BF16)
    return high, (value - high.astype(F32)).astype(BF16)


def split3(value):
    high = value.astype(BF16)
    middle, low = split(value - high.astype(F32))
    return high, middle, low


def stack_left(value):
    h, m, l = split3(value)
    return jnp.concatenate([h, h, m, h, m, l], axis=1)


def stack_right(value):
    h, m, l = split3(value)
    return jnp.concatenate([h, m, h, l, m, h], axis=0)


def dot_t(a, b):
    return lax.dot_general(a, b, (((1,), (1,)), ((), ())), preferred_element_type=F32)


def inverse_factor(gram):
    rows = lax.broadcasted_iota(jnp.int32, (RANK, 4 * RANK), 0)
    lanes = lax.broadcasted_iota(jnp.int32, (RANK, 4 * RANK), 1)
    work = jnp.where(lanes == rows + RANK, 1.0, 0.0)
    work = work + jnp.concatenate([gram, jnp.zeros((RANK, 3 * RANK), F32)], axis=1)
    for k in range(RANK):
        row = work[k : k + 1, :]
        pivot = work[k : k + 1, k : k + 1]
        column = work[:, k : k + 1]
        scale = lax.rsqrt(pivot)
        row = row * scale
        step = work - (column * scale) * row
        below = rows > k
        work = jnp.where(below, step, jnp.where(rows == k, row, work))
    return work[:, RANK : 2 * RANK]


def reduce_kernel(
    g_hbm, e_hbm, qt_hbm, merged_out, ag, left_out,
    g_v, e_v, qt_v, high_v, low_v, p_acc, p_loc, p_rs, p_ar, p_all,
    x_src, x_buf, y_buf, z_src, acc, aux, inv_v,
    load_sem, p_send, p_recv, x_send, x_recv, z_send, z_recv, ag_send, agf_recv, agx_recv, ag_recv, aux_recv, inv_sem, y_recv,
):
    dp, mp = lax.axis_index("dp"), lax.axis_index("mp")
    z, x = dp // NX, lax.rem(dp, NX)
    y, core = mp // 2, lax.rem(mp, 2)
    width = g_v.shape[2]
    n_dp = NZ * NX

    def z_peer(i):
        return lax.rem(z + around(i, NZ), NZ)

    def x_peer(i):
        return lax.rem(x + around(i, NX), NX)

    def dp_peer(i):
        return z_peer(i // NX) * NX + x_peer(lax.rem(i, NX))

    def y_peer(i):
        return lax.rem(y + around(i, NMP // 2), NMP // 2)

    def each(n, act):
        lax.fori_loop(0, n, lambda i, c: (act(i), c)[1], 0)

    def send(src, dst, send_sem, recv_sem, dp_to, mp_to):
        pltpu.make_async_remote_copy(
            src_ref=src, dst_ref=dst, send_sem=send_sem, recv_sem=recv_sem,
            device_id=(dp_to, mp_to), device_id_type=MESH,
        ).start()

    def wait_bytes(ref, sem):
        pltpu.make_async_copy(ref, ref, sem).wait()

    def loads(i):
        cols = pl.ds(pl.multiple_of(i * width, 128), width)
        return (
            pltpu.make_async_copy(qt_hbm.at[:, cols], qt_v.at[i], load_sem.at[2, i]),
            pltpu.make_async_copy(g_hbm.at[0, :, cols], g_v.at[i], load_sem.at[0, i]),
            pltpu.make_async_copy(e_hbm.at[0, :, cols], e_v.at[i], load_sem.at[1, i]),
        )

    for i in range(NX):
        for copy in loads(i):
            copy.start()
        if i == 1:
            barrier = pltpu.get_barrier_semaphore()

            @pl.when(core == 1)
            def _():
                @functools.partial(each, n_dp - 1)
                def _(i):
                    pl.semaphore_signal(
                        barrier, inc=1, device_id=(dp_peer(i), mp), device_id_type=MESH
                    )

                @functools.partial(each, NMP // 2)
                def _(i):
                    pl.semaphore_signal(
                        barrier, inc=1, device_id=(dp, y_peer(i) * 2), device_id_type=MESH
                    )

                @functools.partial(each, NMP // 2 - 1)
                def _(i):
                    pl.semaphore_signal(
                        barrier, inc=1, device_id=(dp, y_peer(i) * 2 + 1), device_id_type=MESH
                    )

            @pl.when(core == 0)
            def _():
                @functools.partial(each, NMP // 2)
                def _(i):
                    pl.semaphore_signal(
                        barrier, inc=1, device_id=(dp, y_peer(i) * 2 + 1), device_id_type=MESH
                    )


    p_acc[...] = jnp.zeros_like(p_acc)

    @functools.partial(each, NX)
    def _(i):
        for copy in loads(i):
            copy.wait()
        merged = g_v[i].astype(F32) + e_v[i]
        merged_out[i] = merged
        high, low = split(merged)
        high_v[i] = high
        low_v[i] = low
        q_both = jnp.concatenate(split(qt_v[i]), axis=0)
        p_acc[...] += dot_t(high, q_both) + dot_t(low, q_both)

    p_t = (p_acc[:, :RANK] + p_acc[:, RANK:]).T
    for t in range(NMP // 2):
        p_loc[t] = p_t[16 * (t % 2) : 16 * (t % 2) + 16, 128 * (t // 2) : 128 * (t // 2) + 128]

    @pl.when(core == 1)
    def _():
        pl.semaphore_wait(barrier, n_dp - 1 + NMP - 1)

    @pl.when(core == 0)
    def _():
        pl.semaphore_wait(barrier, NMP // 2)

    ys = NMP // 2

    def scatter(i):
        to = y_peer(i)
        send(p_loc.at[to], p_rs.at[mp], p_send.at[0], p_recv.at[0], dp, to * 2 + 1)

    def gather(i, c):
        send(p_all.at[y], p_all.at[y], p_send.at[2], p_recv.at[2], dp, y_peer(i) * 2 + c)

    @pl.when(core == 0)
    def _():
        each(ys, scatter)
        wait_bytes(p_all.at[pl.ds(0, ys)], p_recv.at[2])

    @pl.when(core == 1)
    def _():
        each(ys - 1, scatter)
        p_rs[mp] = p_loc[y]
        wait_bytes(p_rs.at[pl.ds(0, NMP - 1)], p_recv.at[0])
        p_ar[dp] = jnp.sum(p_rs[...], axis=0)

        @functools.partial(each, n_dp - 1)
        def _(i):
            send(p_ar.at[dp], p_ar.at[dp], p_send.at[1], p_recv.at[1], dp_peer(i), mp)

        wait_bytes(p_ar.at[pl.ds(0, n_dp - 1)], p_recv.at[1])
        p_all[y] = jnp.sum(p_ar[...], axis=0)
        each(ys, lambda i: gather(i, 0))
        each(ys - 1, lambda i: gather(i, 1))
        wait_bytes(p_all.at[pl.ds(0, ys - 1)], p_recv.at[2])

    p_t = jnp.concatenate(
        [
            jnp.concatenate([p_all[0], p_all[1]], axis=0),
            jnp.concatenate([p_all[2], p_all[3]], axis=0),
        ],
        axis=1,
    )

    p_both = jnp.concatenate(split(p_t), axis=0)
    rows = RANK // NZ

    def compute(to):
        both = jnp.dot(p_both, high_v[to], preferred_element_type=F32)
        both += jnp.dot(p_both, low_v[to], preferred_element_type=F32)
        block = both[:RANK] + both[RANK:]
        for i in range(NZ):
            x_src[to, lax.rem(i - z + NZ, NZ)] = block[i * rows : (i + 1) * rows]

    @functools.partial(each, NX)
    def _(i):
        to = x_peer(i)
        compute(to)

        def pairs(buf, sem):
            for f in (0, 2):
                pair = x_src.at[to, pl.ds(2 + f + f // 2, 2)]
                send(pair, buf.at[x, pl.ds(f, 2)], x_send, sem, z * NX + to, y * 2 + 1)

        @pl.when(core == 0)
        def _():
            pairs(y_buf, y_recv)

        @pl.when(jnp.logical_and(core == 1, i < NX - 1))
        def _():
            pairs(x_buf, x_recv)

    def direct(r, slot, n):
        @functools.partial(each, n)
        def _(i):
            to = x_peer(i)
            send(
                x_src.at[to, r], acc.at[slot + x], z_send, z_recv, lax.rem(z + r, NZ) * NX + to, mp
            )

    for d in (1, 0, 2):
        direct(1 + 3 * d, 4 + 4 * d, NX)
    direct(0, 16, NX - 1)
    acc[16 + x] = x_src[x, 0]

    def factor():
        gram = lax.dot_general(
            p_t, p_t, (((1,), (1,)), ((), ())), precision=HIGHEST, preferred_element_type=F32
        )
        inverse = inverse_factor(gram)
        return inverse

    def project(inverse):
        left_out[ROWS:] = stack_left(inverse * (1.0 / n_dp))
        p_hat = jnp.dot(inverse, p_t, precision=HIGHEST, preferred_element_type=F32).T
        onto = jnp.dot(p_hat, inverse, precision=HIGHEST, preferred_element_type=F32)
        left_out[:ROWS] = stack_left(onto * (1.0 / n_dp))

    def pass_on(buf, c):
        for f in (1, 2, 0, 3):
            z_src[c, f] = jnp.sum(buf[:, f], axis=0)
            to = lax.rem(z + 2 + f + f // 2, NZ)
            send(z_src.at[c, f], acc.at[f], z_send, z_recv, to * NX + x, y * 2 + c)

    @pl.when(core == 1)
    def _():
        for f in (0, 2):
            x_buf[x, f : f + 2] = x_src[x, 2 + f + f // 2 : 4 + f + f // 2]
        wait_bytes(x_buf.at[pl.ds(0, NX - 1)], x_recv)
        pass_on(x_buf, 1)
        wait_bytes(y_buf, y_recv)
        pass_on(y_buf, 0)

    wait_bytes(acc.at[pl.ds(0, 19)], z_recv)
    own = x * NZ + z
    ag[own] = jnp.sum(acc[...], axis=0)

    near, far = (2, 6, 1, 7), (3, 5)

    def spread(src, piece, r, j, c, sem):
        to = lax.rem(z + r, NZ) * NX + lax.rem(x + j, NX)
        send(src, ag.at[piece], ag_send, sem, to, y * 2 + c)

    @pl.when(core == 0)
    def _():
        for j in (2, 1, 3):
            to = z * NX + lax.rem(x + j, NX)
            send(ag.at[own], aux.at[j - 1], ag_send, aux_recv.at[j - 1], to, mp + 1)
        for f, r in enumerate(far):
            to = lax.rem(z + r, NZ) * NX + x
            send(ag.at[own], aux.at[3 + f], ag_send, aux_recv.at[3 + f], to, mp + 1)
        for j in (0, 2, 1, 3):
            spread(ag.at[own], own, 4, j, 0, ag_recv)
        for r in near:
            spread(ag.at[own], own, r, 0, 0, ag_recv)
        inverse = factor()
        inv_v[...] = jnp.concatenate([inverse, jnp.zeros((RANK, 3 * RANK), F32)], axis=1)
        send(inv_v, inv_v, inv_sem.at[0], inv_sem.at[1], dp, mp + 1)
        project(inverse)
        wait_bytes(ag.at[pl.ds(0, n_dp - 1)], ag_recv)
        wait_bytes(ag.at[pl.ds(0, 13)], ag_send)
        wait_bytes(inv_v, inv_sem.at[0])

    @pl.when(core == 1)
    def _():
        for j in (2, 1, 3):
            spread(ag.at[own], own, 0, j, 1, agx_recv.at[j])
        for f, r in enumerate(far):
            spread(ag.at[own], own, r, 0, 1, agf_recv.at[f])
        for j in (0, 2, 1, 3):
            spread(ag.at[own], own, 4, j, 1, ag_recv)
        for r in near:
            spread(ag.at[own], own, r, 0, 1, ag_recv)
        for j in (1, 3, 2):
            piece = lax.rem(x + NX - j, NX) * NZ + z
            wait_bytes(ag.at[piece], agx_recv.at[j])
            for r in near:
                spread(ag.at[piece], piece, r, 0, 1, ag_recv)
        for f, r in enumerate(far):
            piece = x * NZ + lax.rem(z + NZ - r, NZ)
            wait_bytes(ag.at[piece], agf_recv.at[f])
            for j in (2, 1, 3):
                spread(ag.at[piece], piece, 0, j, 1, ag_recv)
        for j in (1, 3, 2):
            piece = lax.rem(x + NX - j, NX) * NZ + z
            wait_bytes(aux.at[j - 1], aux_recv.at[j - 1])
            for r in near + (0,):
                spread(aux.at[j - 1], piece, r, 0, 0, ag_recv)
        for f, r in enumerate(far):
            piece = x * NZ + lax.rem(z + NZ - r, NZ)
            wait_bytes(aux.at[3 + f], aux_recv.at[3 + f])
            for j in (2, 1, 3, 0):
                spread(aux.at[3 + f], piece, 0, j, 0, ag_recv)
        wait_bytes(inv_v, inv_sem.at[1])
        project(inv_v[:, :RANK])
        wait_bytes(ag.at[pl.ds(0, n_dp - 6)], ag_recv)
        wait_bytes(ag.at[pl.ds(0, n_dp - 1)], ag_send)
        wait_bytes(ag.at[pl.ds(0, 23)], ag_send)

    @pl.when(core == 0)
    def _():
        wait_bytes(p_rs.at[pl.ds(0, ys)], p_send.at[0])
        wait_bytes(x_buf, x_send)
        wait_bytes(acc.at[pl.ds(0, 15)], z_send)

    @pl.when(core == 1)
    def _():
        wait_bytes(p_rs.at[pl.ds(0, ys - 1)], p_send.at[0])
        wait_bytes(x_buf.at[pl.ds(0, NX - 1)], x_send)
        wait_bytes(ag.at[pl.ds(0, 23)], z_send)
        wait_bytes(p_ar.at[pl.ds(0, n_dp - 1)], p_send.at[1])
        wait_bytes(p_rs.at[pl.ds(0, NMP - 1)], p_send.at[2])


def finish_kernel(merged_ref, q_ref, left_ref, u_hbm, n_hbm, q_hbm, u_v, n_v, q_v, sems):
    blocks, _, width = merged_ref.shape
    half = ROWS // 2

    def block(i, carry):
        cols = pl.ds(pl.multiple_of(i * width, 128), width)
        right = stack_right(jnp.concatenate([q_ref[i * NZ + j] for j in range(NZ)], axis=0))
        for h in range(2):
            rows = slice(h * half, (h + 1) * half)
            at = pl.ds(h * half, half)
            recon = jnp.dot(left_ref[rows], right, preferred_element_type=F32)
            n_v[i, rows] = merged_ref[i, rows] - recon
            pltpu.make_async_copy(n_v.at[i, at], n_hbm.at[0, at, cols], sems.at[1]).start()
            u_v[i, rows] = recon.astype(BF16)
            pltpu.make_async_copy(u_v.at[i, at], u_hbm.at[at, cols], sems.at[2]).start()
        q_v[i] = jnp.dot(left_ref[ROWS:], right, preferred_element_type=F32)
        pltpu.make_async_copy(q_v.at[i], q_hbm.at[:, cols], sems.at[0]).start()
        return carry

    lax.fori_loop(0, blocks, block, 0)
    for ref, sem in ((q_v, sems.at[0]), (n_v, sems.at[1]), (u_v, sems.at[2])):
        pltpu.make_async_copy(ref, ref, sem).wait()


def body(grads, errors, q_init):
    columns = grads.shape[2]
    width = columns // NX
    piece = RANK // NZ
    dma = pltpu.SemaphoreType.DMA
    held = pl.pallas_call(
        reduce_kernel,
        out_shape=(
            jax.ShapeDtypeStruct((NX, ROWS, width), F32),
            jax.ShapeDtypeStruct((NX * NZ, piece, width), F32),
            jax.ShapeDtypeStruct((ROWS + RANK, 6 * RANK), BF16),
        ),
        in_specs=[HBM] * 3,
        out_specs=[VMEM] * 3,
        scratch_shapes=[
            pltpu.VMEM((NX, ROWS, width), BF16),
            pltpu.VMEM((NX, ROWS, width), F32),
            pltpu.VMEM((NX, RANK, width), F32),
            pltpu.VMEM((NX, ROWS, width), BF16),
            pltpu.VMEM((NX, ROWS, width), BF16),
            pltpu.VMEM((ROWS, 2 * RANK), F32),
            pltpu.VMEM((NMP // 2, 16, 128), F32),
            pltpu.VMEM((NMP, 16, 128), F32),
            pltpu.VMEM((NZ * NX, 16, 128), F32),
            pltpu.VMEM((NMP // 2, 16, 128), F32),
            pltpu.VMEM((NX, NZ, piece, width), F32),
            pltpu.VMEM((NX, 4, piece, width), F32),
            pltpu.VMEM((NX, 4, piece, width), F32),
            pltpu.VMEM((2, 4, piece, width), F32),
            pltpu.VMEM((20, piece, width), F32),
            pltpu.VMEM((5, piece, width), F32),
            pltpu.VMEM((RANK, 4 * RANK), F32),
            dma((3, NX)),
            dma((3,)),
            dma((3,)),
            dma,
            dma,
            dma,
            dma,
            dma,
            dma((2,)),
            dma((NX,)),
            dma,
            dma((5,)),
            dma((2,)),
            dma,
        ],
        compiler_params=pltpu.CompilerParams(
            collective_id=0, has_side_effects=True, vmem_limit_bytes=40 << 20
        ),
        name="reduce",
    )(*(pltpu.with_memory_space_constraint(a, pltpu.HBM) for a in (grads, errors, q_init.T)))

    update, new_errors, q_next = pl.pallas_call(
        finish_kernel,
        out_shape=(
            jax.ShapeDtypeStruct((ROWS, columns), BF16),
            jax.ShapeDtypeStruct((1, ROWS, columns), F32),
            jax.ShapeDtypeStruct((RANK, columns), F32),
        ),
        in_specs=[VMEM] * 3,
        out_specs=[HBM] * 3,
        scratch_shapes=[
            pltpu.VMEM((NX, ROWS, width), BF16),
            pltpu.VMEM((NX, ROWS, width), F32),
            pltpu.VMEM((NX, RANK, width), F32),
            dma((3,)),
        ],
        compiler_params=pltpu.CompilerParams(vmem_limit_bytes=32 << 20),
        name="finish",
    )(*held)
    return (update, new_errors, q_next.T)


def solution(mesh):
    placed = (P("dp", None, "mp"), P("dp", None, "mp"), P("mp", None))
    return jax.shard_map(
        body,
        mesh=mesh,
        in_specs=placed,
        out_specs=(P(None, "mp"), P("dp", None, "mp"), P("mp", None)),
        check_vma=False,
    )
```

```python
import functools

import jax
import jax.numpy as jnp
from jax import lax
from jax.experimental import pallas as pl
from jax.experimental.pallas import tpu as pltpu
from jax.sharding import PartitionSpec as P

MESH = pl.DeviceIdType.MESH
HIGHEST = lax.Precision.HIGHEST
F32 = jnp.float32
BF16 = jnp.bfloat16

NZ, NX, NMP = 8, 4, 8
ROWS, RANK = 256, 32
VMEM = pl.BlockSpec(memory_space=pltpu.VMEM)
HBM = pl.BlockSpec(memory_space=pltpu.HBM)


def around(i, size):
    half = (i + 1) // 2
    return lax.rem(size // 2 + jnp.where(lax.rem(i, 2) == 0, half, size - half), size)


def split(value):
    high = value.astype(BF16)
    return high, (value - high.astype(F32)).astype(BF16)


def split3(value):
    high = value.astype(BF16)
    middle, low = split(value - high.astype(F32))
    return high, middle, low


def stack_left(value):
    h, m, l = split3(value)
    return jnp.concatenate([h, h, m, h, m, l], axis=1)


def stack_right(value):
    h, m, l = split3(value)
    return jnp.concatenate([h, m, h, l, m, h], axis=0)


def dot_t(a, b):
    return lax.dot_general(a, b, (((1,), (1,)), ((), ())), preferred_element_type=F32)


def inverse_factor(gram):
    rows = lax.broadcasted_iota(jnp.int32, (RANK, 4 * RANK), 0)
    lanes = lax.broadcasted_iota(jnp.int32, (RANK, 4 * RANK), 1)
    work = jnp.where(lanes == rows + RANK, 1.0, 0.0)
    work = work + jnp.concatenate([gram, jnp.zeros((RANK, 3 * RANK), F32)], axis=1)
    for k in range(RANK):
        row = work[k : k + 1, :]
        pivot = work[k : k + 1, k : k + 1]
        column = work[:, k : k + 1]
        scale = lax.rsqrt(pivot)
        row = row * scale
        step = work - (column * scale) * row
        below = rows > k
        work = jnp.where(below, step, jnp.where(rows == k, row, work))
    return work[:, RANK : 2 * RANK]


def reduce_kernel(
    g_hbm, e_hbm, qt_hbm, merged_out, ag, left_out,
    g_v, e_v, qt_v, high_v, low_v, p_acc, p_loc, p_rs, p_ar, p_all,
    x_src, x_buf, y_buf, z_src, acc, aux, inv_v,
    load_sem, p_send, p_recv, x_send, x_recv, z_send, z_recv, ag_send, agf_recv, agx_recv, ag_recv, aux_recv, inv_sem, y_recv,
):
    dp, mp = lax.axis_index("dp"), lax.axis_index("mp")
    z, x = dp // NX, lax.rem(dp, NX)
    y, core = mp // 2, lax.rem(mp, 2)
    width = g_v.shape[2]
    n_dp = NZ * NX

    def z_peer(i):
        return lax.rem(z + around(i, NZ), NZ)

    def x_peer(i):
        return lax.rem(x + around(i, NX), NX)

    def dp_peer(i):
        return z_peer(i // NX) * NX + x_peer(lax.rem(i, NX))

    def y_peer(i):
        return lax.rem(y + around(i, NMP // 2), NMP // 2)

    def each(n, act):
        lax.fori_loop(0, n, lambda i, c: (act(i), c)[1], 0)

    def send(src, dst, send_sem, recv_sem, dp_to, mp_to):
        pltpu.make_async_remote_copy(
            src_ref=src, dst_ref=dst, send_sem=send_sem, recv_sem=recv_sem,
            device_id=(dp_to, mp_to), device_id_type=MESH,
        ).start()

    def wait_bytes(ref, sem):
        pltpu.make_async_copy(ref, ref, sem).wait()

    def loads(i):
        cols = pl.ds(pl.multiple_of(i * width, 128), width)
        return (
            pltpu.make_async_copy(qt_hbm.at[:, cols], qt_v.at[i], load_sem.at[2, i]),
            pltpu.make_async_copy(g_hbm.at[0, :, cols], g_v.at[i], load_sem.at[0, i]),
            pltpu.make_async_copy(e_hbm.at[0, :, cols], e_v.at[i], load_sem.at[1, i]),
        )

    for i in range(NX):
        for copy in loads(i):
            copy.start()
        if i == NX - 1:
            barrier = pltpu.get_barrier_semaphore()

            @pl.when(core == 1)
            def _():
                @functools.partial(each, n_dp - 1)
                def _(i):
                    pl.semaphore_signal(
                        barrier, inc=1, device_id=(dp_peer(i), mp), device_id_type=MESH
                    )

                @functools.partial(each, NMP // 2)
                def _(i):
                    pl.semaphore_signal(
                        barrier, inc=1, device_id=(dp, y_peer(i) * 2), device_id_type=MESH
                    )

                @functools.partial(each, NMP // 2 - 1)
                def _(i):
                    pl.semaphore_signal(
                        barrier, inc=1, device_id=(dp, y_peer(i) * 2 + 1), device_id_type=MESH
                    )

            @pl.when(core == 0)
            def _():
                @functools.partial(each, NMP // 2)
                def _(i):
                    pl.semaphore_signal(
                        barrier, inc=1, device_id=(dp, y_peer(i) * 2 + 1), device_id_type=MESH
                    )


    p_acc[...] = jnp.zeros_like(p_acc)

    @functools.partial(each, NX)
    def _(i):
        for copy in loads(i):
            copy.wait()
        merged = g_v[i].astype(F32) + e_v[i]
        merged_out[i] = merged
        high, low = split(merged)
        high_v[i] = high
        low_v[i] = low
        q_both = jnp.concatenate(split(qt_v[i]), axis=0)
        p_acc[...] += dot_t(high, q_both) + dot_t(low, q_both)

    p_t = (p_acc[:, :RANK] + p_acc[:, RANK:]).T
    for t in range(NMP // 2):
        p_loc[t] = p_t[16 * (t % 2) : 16 * (t % 2) + 16, 128 * (t // 2) : 128 * (t // 2) + 128]

    @pl.when(core == 1)
    def _():
        pl.semaphore_wait(barrier, n_dp - 1 + NMP - 1)

    @pl.when(core == 0)
    def _():
        pl.semaphore_wait(barrier, NMP // 2)

    ys = NMP // 2

    def scatter(i):
        to = y_peer(i)
        send(p_loc.at[to], p_rs.at[mp], p_send.at[0], p_recv.at[0], dp, to * 2 + 1)

    def gather(i, c):
        send(p_all.at[y], p_all.at[y], p_send.at[2], p_recv.at[2], dp, y_peer(i) * 2 + c)

    @pl.when(core == 0)
    def _():
        each(ys, scatter)
        wait_bytes(p_all.at[pl.ds(0, ys)], p_recv.at[2])

    @pl.when(core == 1)
    def _():
        each(ys - 1, scatter)
        p_rs[mp] = p_loc[y]
        wait_bytes(p_rs.at[pl.ds(0, NMP - 1)], p_recv.at[0])
        p_ar[dp] = jnp.sum(p_rs[...], axis=0)

        @functools.partial(each, n_dp - 1)
        def _(i):
            send(p_ar.at[dp], p_ar.at[dp], p_send.at[1], p_recv.at[1], dp_peer(i), mp)

        wait_bytes(p_ar.at[pl.ds(0, n_dp - 1)], p_recv.at[1])
        p_all[y] = jnp.sum(p_ar[...], axis=0)
        each(ys, lambda i: gather(i, 0))
        each(ys - 1, lambda i: gather(i, 1))
        wait_bytes(p_all.at[pl.ds(0, ys - 1)], p_recv.at[2])

    p_t = jnp.concatenate(
        [
            jnp.concatenate([p_all[0], p_all[1]], axis=0),
            jnp.concatenate([p_all[2], p_all[3]], axis=0),
        ],
        axis=1,
    )

    p_both = jnp.concatenate(split(p_t), axis=0)
    rows = RANK // NZ

    def compute(to):
        both = jnp.dot(p_both, high_v[to], preferred_element_type=F32)
        both += jnp.dot(p_both, low_v[to], preferred_element_type=F32)
        block = both[:RANK] + both[RANK:]
        for i in range(NZ):
            x_src[to, lax.rem(i - z + NZ, NZ)] = block[i * rows : (i + 1) * rows]

    @functools.partial(each, NX)
    def _(i):
        to = x_peer(i)
        compute(to)

        def pairs(buf, sem):
            for f in (0, 2):
                pair = x_src.at[to, pl.ds(2 + f + f // 2, 2)]
                send(pair, buf.at[x, pl.ds(f, 2)], x_send, sem, z * NX + to, y * 2 + 1)

        @pl.when(core == 0)
        def _():
            pairs(y_buf, y_recv)

        @pl.when(jnp.logical_and(core == 1, i < NX - 1))
        def _():
            pairs(x_buf, x_recv)

    def direct(r, slot, n):
        @functools.partial(each, n)
        def _(i):
            to = x_peer(i)
            send(
                x_src.at[to, r], acc.at[slot + x], z_send, z_recv, lax.rem(z + r, NZ) * NX + to, mp
            )

    for d in (1, 0, 2):
        direct(1 + 3 * d, 4 + 4 * d, NX)
    direct(0, 16, NX - 1)
    acc[16 + x] = x_src[x, 0]

    def factor():
        gram = lax.dot_general(
            p_t, p_t, (((1,), (1,)), ((), ())), precision=HIGHEST, preferred_element_type=F32
        )
        inverse = inverse_factor(gram)
        return inverse

    def project(inverse):
        left_out[ROWS:] = stack_left(inverse * (1.0 / n_dp))
        p_hat = jnp.dot(inverse, p_t, precision=HIGHEST, preferred_element_type=F32).T
        onto = jnp.dot(p_hat, inverse, precision=HIGHEST, preferred_element_type=F32)
        left_out[:ROWS] = stack_left(onto * (1.0 / n_dp))

    def pass_on(buf, c):
        for f in (1, 2, 0, 3):
            z_src[c, f] = jnp.sum(buf[:, f], axis=0)
            to = lax.rem(z + 2 + f + f // 2, NZ)
            send(z_src.at[c, f], acc.at[f], z_send, z_recv, to * NX + x, y * 2 + c)

    @pl.when(core == 1)
    def _():
        for f in (0, 2):
            x_buf[x, f : f + 2] = x_src[x, 2 + f + f // 2 : 4 + f + f // 2]
        wait_bytes(x_buf.at[pl.ds(0, NX - 1)], x_recv)
        pass_on(x_buf, 1)
        wait_bytes(y_buf, y_recv)
        pass_on(y_buf, 0)

    wait_bytes(acc.at[pl.ds(0, 19)], z_recv)
    own = x * NZ + z
    ag[own] = jnp.sum(acc[...], axis=0)

    near, far = (2, 6, 1, 7), (3, 5)

    def spread(src, piece, r, j, c, sem):
        to = lax.rem(z + r, NZ) * NX + lax.rem(x + j, NX)
        send(src, ag.at[piece], ag_send, sem, to, y * 2 + c)

    @pl.when(core == 0)
    def _():
        for f, r in enumerate(far):
            to = lax.rem(z + r, NZ) * NX + x
            send(ag.at[own], aux.at[3 + f], ag_send, aux_recv.at[3 + f], to, mp + 1)
        for j in (2, 1, 3):
            to = z * NX + lax.rem(x + j, NX)
            send(ag.at[own], aux.at[j - 1], ag_send, aux_recv.at[j - 1], to, mp + 1)
        for j in (0, 2, 1, 3):
            spread(ag.at[own], own, 4, j, 0, ag_recv)
        for r in near:
            spread(ag.at[own], own, r, 0, 0, ag_recv)
        inverse = factor()
        inv_v[...] = jnp.concatenate([inverse, jnp.zeros((RANK, 3 * RANK), F32)], axis=1)
        send(inv_v, inv_v, inv_sem.at[0], inv_sem.at[1], dp, mp + 1)
        project(inverse)
        wait_bytes(ag.at[pl.ds(0, n_dp - 1)], ag_recv)
        wait_bytes(ag.at[pl.ds(0, 13)], ag_send)
        wait_bytes(inv_v, inv_sem.at[0])

    @pl.when(core == 1)
    def _():
        for j in (2, 1, 3):
            spread(ag.at[own], own, 0, j, 1, agx_recv.at[j])
        for f, r in enumerate(far):
            spread(ag.at[own], own, r, 0, 1, agf_recv.at[f])
        for j in (0, 2, 1, 3):
            spread(ag.at[own], own, 4, j, 1, ag_recv)
        for r in near:
            spread(ag.at[own], own, r, 0, 1, ag_recv)
        for j in (1, 3, 2):
            piece = lax.rem(x + NX - j, NX) * NZ + z
            wait_bytes(ag.at[piece], agx_recv.at[j])
            for r in near:
                spread(ag.at[piece], piece, r, 0, 1, ag_recv)
        for j in (1, 3, 2):
            piece = lax.rem(x + NX - j, NX) * NZ + z
            wait_bytes(aux.at[j - 1], aux_recv.at[j - 1])
            for r in near + (0,):
                spread(aux.at[j - 1], piece, r, 0, 0, ag_recv)
        for f, r in enumerate(far):
            piece = x * NZ + lax.rem(z + NZ - r, NZ)
            wait_bytes(ag.at[piece], agf_recv.at[f])
            for j in (2, 1, 3):
                spread(ag.at[piece], piece, 0, j, 1, ag_recv)
        for f, r in enumerate(far):
            piece = x * NZ + lax.rem(z + NZ - r, NZ)
            wait_bytes(aux.at[3 + f], aux_recv.at[3 + f])
            for j in (2, 1, 3, 0):
                spread(aux.at[3 + f], piece, 0, j, 0, ag_recv)
        wait_bytes(inv_v, inv_sem.at[1])
        project(inv_v[:, :RANK])
        wait_bytes(ag.at[pl.ds(0, n_dp - 6)], ag_recv)
        wait_bytes(ag.at[pl.ds(0, n_dp - 1)], ag_send)
        wait_bytes(ag.at[pl.ds(0, 23)], ag_send)

    @pl.when(core == 0)
    def _():
        wait_bytes(p_rs.at[pl.ds(0, ys)], p_send.at[0])
        wait_bytes(x_buf, x_send)
        wait_bytes(acc.at[pl.ds(0, 15)], z_send)

    @pl.when(core == 1)
    def _():
        wait_bytes(p_rs.at[pl.ds(0, ys - 1)], p_send.at[0])
        wait_bytes(x_buf.at[pl.ds(0, NX - 1)], x_send)
        wait_bytes(ag.at[pl.ds(0, 23)], z_send)
        wait_bytes(p_ar.at[pl.ds(0, n_dp - 1)], p_send.at[1])
        wait_bytes(p_rs.at[pl.ds(0, NMP - 1)], p_send.at[2])


def finish_kernel(merged_ref, q_ref, left_ref, u_hbm, n_hbm, q_hbm, u_v, n_v, q_v, sems):
    blocks, _, width = merged_ref.shape
    half = ROWS // 2

    def block(i, carry):
        cols = pl.ds(pl.multiple_of(i * width, 128), width)
        right = stack_right(jnp.concatenate([q_ref[i * NZ + j] for j in range(NZ)], axis=0))
        for h in range(2):
            rows = slice(h * half, (h + 1) * half)
            at = pl.ds(h * half, half)
            recon = jnp.dot(left_ref[rows], right, preferred_element_type=F32)
            n_v[i, rows] = merged_ref[i, rows] - recon
            pltpu.make_async_copy(n_v.at[i, at], n_hbm.at[0, at, cols], sems.at[1]).start()
            u_v[i, rows] = recon.astype(BF16)
            pltpu.make_async_copy(u_v.at[i, at], u_hbm.at[at, cols], sems.at[2]).start()
        q_v[i] = jnp.dot(left_ref[ROWS:], right, preferred_element_type=F32)
        pltpu.make_async_copy(q_v.at[i], q_hbm.at[:, cols], sems.at[0]).start()
        return carry

    lax.fori_loop(0, blocks, block, 0)
    for ref, sem in ((q_v, sems.at[0]), (n_v, sems.at[1]), (u_v, sems.at[2])):
        pltpu.make_async_copy(ref, ref, sem).wait()


def body(grads, errors, q_init):
    columns = grads.shape[2]
    width = columns // NX
    piece = RANK // NZ
    dma = pltpu.SemaphoreType.DMA
    held = pl.pallas_call(
        reduce_kernel,
        out_shape=(
            jax.ShapeDtypeStruct((NX, ROWS, width), F32),
            jax.ShapeDtypeStruct((NX * NZ, piece, width), F32),
            jax.ShapeDtypeStruct((ROWS + RANK, 6 * RANK), BF16),
        ),
        in_specs=[HBM] * 3,
        out_specs=[VMEM] * 3,
        scratch_shapes=[
            pltpu.VMEM((NX, ROWS, width), BF16),
            pltpu.VMEM((NX, ROWS, width), F32),
            pltpu.VMEM((NX, RANK, width), F32),
            pltpu.VMEM((NX, ROWS, width), BF16),
            pltpu.VMEM((NX, ROWS, width), BF16),
            pltpu.VMEM((ROWS, 2 * RANK), F32),
            pltpu.VMEM((NMP // 2, 16, 128), F32),
            pltpu.VMEM((NMP, 16, 128), F32),
            pltpu.VMEM((NZ * NX, 16, 128), F32),
            pltpu.VMEM((NMP // 2, 16, 128), F32),
            pltpu.VMEM((NX, NZ, piece, width), F32),
            pltpu.VMEM((NX, 4, piece, width), F32),
            pltpu.VMEM((NX, 4, piece, width), F32),
            pltpu.VMEM((2, 4, piece, width), F32),
            pltpu.VMEM((20, piece, width), F32),
            pltpu.VMEM((5, piece, width), F32),
            pltpu.VMEM((RANK, 4 * RANK), F32),
            dma((3, NX)),
            dma((3,)),
            dma((3,)),
            dma,
            dma,
            dma,
            dma,
            dma,
            dma((2,)),
            dma((NX,)),
            dma,
            dma((5,)),
            dma((2,)),
            dma,
        ],
        compiler_params=pltpu.CompilerParams(
            collective_id=0, has_side_effects=True, vmem_limit_bytes=40 << 20
        ),
        name="reduce",
    )(*(pltpu.with_memory_space_constraint(a, pltpu.HBM) for a in (grads, errors, q_init.T)))

    update, new_errors, q_next = pl.pallas_call(
        finish_kernel,
        out_shape=(
            jax.ShapeDtypeStruct((ROWS, columns), BF16),
            jax.ShapeDtypeStruct((1, ROWS, columns), F32),
            jax.ShapeDtypeStruct((RANK, columns), F32),
        ),
        in_specs=[VMEM] * 3,
        out_specs=[HBM] * 3,
        scratch_shapes=[
            pltpu.VMEM((NX, ROWS, width), BF16),
            pltpu.VMEM((NX, ROWS, width), F32),
            pltpu.VMEM((NX, RANK, width), F32),
            dma((3,)),
        ],
        compiler_params=pltpu.CompilerParams(vmem_limit_bytes=32 << 20),
        name="finish",
    )(*held)
    return (update, new_errors, q_next.T)


def solution(mesh):
    placed = (P("dp", None, "mp"), P("dp", None, "mp"), P("mp", None))
    return jax.shard_map(
        body,
        mesh=mesh,
        in_specs=placed,
        out_specs=(P(None, "mp"), P("dp", None, "mp"), P("mp", None)),
        check_vma=False,
    )
```
